512 devices in a mesh: lon: 128 (over z_hi, x, y, core), lev: 4 (over z_lo).
Axes of the slice: x: 4, y: 8, z: 8 (z_hi: 2, z_lo: 4; z = z_hi * 4 + z_lo), core: 2. Of those that a mesh axis runs over, the one named last changes fastest.
Arguments:
- latents: bfloat16 [2, 24, 3072, 512], P(None, 'lev', 'lon'), may hold values from -120 to 120
- shift_offset: int32 [1], replicated, may hold values from 1 to 11
- qkv_weight: bfloat16 [512, 1536], replicated, may hold values from -0.25 to 0.25
- proj_weight: bfloat16 [512, 512], replicated, may hold values from -0.25 to 0.25
- post_gain: float32 [512], replicated, may hold values from 0.5 to 1.5
- bias_first_weight: float32 [3, 512], replicated, may hold values from -6 to 6
- bias_first_offset: float32 [512], replicated, may hold values from -3 to 3
- bias_second_weight: float32 [512, 16], replicated, may hold values from -0.25 to 0.25
- dec_gain: float32 [512], replicated, may hold values from 0.5 to 1.5
- kv_weight: bfloat16 [512, 1024], replicated, may hold values from -0.25 to 0.25
- head_weight: bfloat16 [512, 80], replicated, may hold values from -0.25 to 0.25
- level_queries: float32 [8, 512], replicated, may hold values from -120 to 120
- level_order: int32 [8], replicated, may hold values from 0 to 7, each once
Outputs:
- hidden_state_out: bfloat16 [2, 24, 3072, 512], P(None, 'lev', 'lon')
- predicted_tiles: bfloat16 [8, 24, 245760], P('lev', None, 'lon')
The draws below stay inside these ranges and needn't reach their ends.
Inputs may be any that keep to these rules, and one draw needn't show every extreme that they name: `level_order`: each of 0 to 7 exactly once.
All inputs are finite; a program needn't handle non-finite values.
Results may differ from the reference program's by a relative error of at most 0.017.
Values may be sent and summed in bfloat16 or wider, within the bound.
A program may use at most 128 MiB of HBM per device.

```python
import math
import jax
import jax.numpy as jnp
import numpy as np
from jax import lax

D = 512
HEAD_TOTAL = 16
BIAS_NET_UNITS = 512
Z = 2
MERIDIAN_TILES = 24
ZONAL_TILES = 3072
ISOBAR_NUMBER = 8
TILE_ENTRIES = 80


def draw_latents(key, part):
    key = jax.random.fold_in(key, 11)
    first = jax.random.fold_in(key, 0)
    values = jnp.clip(jax.random.normal(first, (Z, MERIDIAN_TILES, ZONAL_TILES, D), jnp.float32), -6.0, 6.0)
    return values.astype(jnp.bfloat16)


def draw_level_queries(key, part):
    key = jax.random.fold_in(key, 23)
    first = jax.random.fold_in(key, 0)
    values = jnp.clip(jax.random.normal(first, (ISOBAR_NUMBER, D), jnp.float32), -6.0, 6.0)
    return values


def scatter_about(own_key, extent, width, bound, kind=jnp.bfloat16):
    values = width * jax.random.normal(own_key, extent, jnp.float32)
    return jnp.clip(values, min=-bound, max=bound).astype(kind)


def setup_inputs(seed: int = 0) -> dict:
    seeds = jax.random.split(jax.random.key(seed), 14)
    return {
        "latents": draw_latents(jax.random.fold_in(seeds[13], 71), 0),
        "shift_offset": jax.random.randint(seeds[1], (1,), 1, 12).astype(jnp.int32),
        "qkv_weight": scatter_about(seeds[2], (D, 3 * D), D ** -0.5, 0.25),
        "proj_weight": scatter_about(seeds[3], (D, D), D ** -0.5, 0.25),
        "post_gain": jnp.clip(1.0 + 0.1 * jax.random.normal(seeds[4], (D,), jnp.float32), 0.5, 1.5),
        "bias_first_weight": scatter_about(seeds[5], (3, BIAS_NET_UNITS), 1.0, 6.0, jnp.float32),
        "bias_first_offset": scatter_about(seeds[6], (BIAS_NET_UNITS,), 0.5, 3.0, jnp.float32),
        "bias_second_weight": scatter_about(seeds[7], (BIAS_NET_UNITS, HEAD_TOTAL), BIAS_NET_UNITS ** -0.5, 0.25, jnp.float32),
        "dec_gain": jnp.clip(1.0 + 0.1 * jax.random.normal(seeds[8], (D,), jnp.float32), 0.5, 1.5),
        "kv_weight": scatter_about(seeds[9], (D, 2 * D), D ** -0.5, 0.25),
        "head_weight": scatter_about(seeds[10], (D, TILE_ENTRIES), D ** -0.5, 0.25),
        "level_queries": draw_level_queries(jax.random.fold_in(seeds[13], 71), 0),
        "level_order": jax.random.permutation(seeds[12], ISOBAR_NUMBER).astype(jnp.int32),
    }


epsilon = 1e-05

def offset_index():
    depth_pos, row_pos, col_pos = np.meshgrid(np.arange(2), np.arange(6), np.arange(12), indexing='ij')
    depth_pos = depth_pos.reshape(-1)
    row_pos = row_pos.reshape(-1)
    col_pos = col_pos.reshape(-1)
    depth_off = depth_pos[:, None] - depth_pos[None, :] + 1
    row_off = row_pos[:, None] - row_pos[None, :] + 5
    col_off = col_pos[:, None] - col_pos[None, :] + 11
    return ((depth_off * 11 + row_off) * 23 + col_off).reshape(-1)

def bias_table(bias_first_weight, bias_first_offset, bias_second_weight):
    depth_off = (jnp.arange(3, dtype=jnp.float32) - 1.0) * 8.0
    row_off = (jnp.arange(11, dtype=jnp.float32) - 5.0) * 8.0 / 5.0
    col_off = (jnp.arange(23, dtype=jnp.float32) - 11.0) * 8.0 / 11.0
    grid_depth, grid_row, grid_col = jnp.meshgrid(depth_off, row_off, col_off, indexing='ij')
    coords = jnp.stack([grid_depth, grid_row, grid_col], axis=-1).reshape(-1, 3)
    coords = jnp.sign(coords) * jnp.log2(jnp.abs(coords) + 1.0) / 3.0
    hidden = jax.nn.relu(jnp.dot(coords, bias_first_weight, precision=lax.Precision.HIGHEST) + bias_first_offset)
    table = 16.0 * jax.nn.sigmoid(jnp.dot(hidden, bias_second_weight, precision=lax.Precision.HIGHEST))
    picked = jnp.take(table, jnp.asarray(offset_index(), dtype=jnp.int32), axis=0)
    return picked.reshape(144, 144, -1).transpose(2, 0, 1)

def layer_norm(values):
    centre = values - lax.optimization_barrier(jnp.mean(values, axis=-1, keepdims=True))
    spread = lax.optimization_barrier(jnp.mean(centre * centre, axis=-1, keepdims=True))
    return centre * lax.rsqrt(spread + epsilon)

def window_block(strip, position_bias, qkv_weight, proj_weight, post_gain):
    depth_count, row_count, col_count, width_all = strip.shape
    head_count = position_bias.shape[0]
    head_dim = width_all // head_count
    windows = strip.reshape(depth_count // 2, 2, row_count // 6, 6, col_count // 12, 12, width_all)
    windows = windows.transpose(0, 2, 4, 1, 3, 5, 6).reshape(-1, 144, width_all)
    window_count = windows.shape[0]
    packed = jnp.einsum('wtc,cf->wtf', windows.astype(jnp.float32), qkv_weight.astype(jnp.float32)).astype(jnp.bfloat16)
    packed = packed.reshape(window_count, 144, 3, head_count, head_dim)
    scores = jnp.einsum('wqhd,wkhd->whqk', packed[:, :, 0].astype(jnp.float32), packed[:, :, 1].astype(jnp.float32))
    scores = scores / math.sqrt(head_dim) + position_bias[None]
    largest = lax.optimization_barrier(jnp.max(scores, axis=-1, keepdims=True))
    raised = jnp.exp(scores - largest)
    probabilities = (raised / lax.optimization_barrier(jnp.sum(raised, axis=-1, keepdims=True))).astype(jnp.bfloat16)
    attended = jnp.einsum('whqk,wkhd->wqhd', probabilities.astype(jnp.float32), packed[:, :, 2].astype(jnp.float32))
    attended = attended.astype(jnp.bfloat16).reshape(window_count, 144, width_all)
    projected = jnp.einsum('wtc,cf->wtf', attended.astype(jnp.float32), proj_weight.astype(jnp.float32))
    blended = (windows.astype(jnp.float32) + post_gain * layer_norm(projected)).astype(jnp.bfloat16)
    blended = blended.reshape(depth_count // 2, row_count // 6, col_count // 12, 2, 6, 12, width_all)
    return blended.transpose(0, 3, 1, 4, 2, 5, 6).reshape(depth_count, row_count, col_count, width_all)

def decode(strip, ordered, dec_gain, kv_weight, head_weight, head_count):
    depth_count, row_count, col_count, width_all = strip.shape
    head_dim = width_all // head_count
    normed = (dec_gain * layer_norm(strip.astype(jnp.float32))).astype(jnp.bfloat16)
    memory = jnp.einsum('zrcd,df->zrcf', normed.astype(jnp.float32), kv_weight.astype(jnp.float32)).astype(jnp.bfloat16)
    key_part = memory[..., :width_all].reshape(depth_count, row_count, col_count, head_count, head_dim)
    value_part = memory[..., width_all:].reshape(depth_count, row_count, col_count, head_count, head_dim).astype(jnp.float32)

    def one_level(level_query):
        query_part = level_query.astype(jnp.bfloat16).reshape(head_count, head_dim)
        scores = jnp.einsum('hd,zrchd->zrch', query_part.astype(jnp.float32), key_part.astype(jnp.float32)) / math.sqrt(head_dim)
        largest = lax.optimization_barrier(jnp.max(scores, axis=0, keepdims=True))
        raised = jnp.exp(scores - largest)
        weights = raised / lax.optimization_barrier(jnp.sum(raised, axis=0, keepdims=True))
        decoded = lax.optimization_barrier(jnp.sum(weights[..., None] * value_part, axis=0)).reshape(row_count, col_count, width_all).astype(jnp.bfloat16)
        result = jnp.einsum('rcd,dp->rcp', decoded.astype(jnp.float32), head_weight.astype(jnp.float32)).astype(jnp.bfloat16)
        return result.reshape(row_count, col_count * head_weight.shape[1])
    return lax.map(one_level, ordered)

def reference(latents, shift_offset, qkv_weight, proj_weight, post_gain, bias_first_weight, bias_first_offset, bias_second_weight, dec_gain, kv_weight, head_weight, level_queries, level_order):
    offset_cols = shift_offset[0]
    position_bias = bias_table(bias_first_weight, bias_first_offset, bias_second_weight)
    rolled = jnp.roll(latents, -offset_cols, axis=2)
    blocks = rolled.reshape(Z, MERIDIAN_TILES, ZONAL_TILES // 12, 12, D).transpose(2, 0, 1, 3, 4)

    def swin_block(strip):
        return window_block(strip, position_bias, qkv_weight, proj_weight, post_gain)
    mixed = lax.map(swin_block, blocks).transpose(1, 2, 0, 3, 4).reshape(Z, MERIDIAN_TILES, ZONAL_TILES, D)
    hidden_state_out = jnp.roll(mixed, offset_cols, axis=2)
    selector = (level_order[:, None] == jnp.arange(ISOBAR_NUMBER, dtype=jnp.int32)[None, :]).astype(jnp.float32)
    ordered = jnp.dot(selector, level_queries, precision=lax.Precision.HIGHEST)
    head_count = bias_second_weight.shape[1]
    out_blocks = hidden_state_out.reshape(Z, MERIDIAN_TILES, ZONAL_TILES // 12, 12, D).transpose(2, 0, 1, 3, 4)

    def decode_block(strip):
        return decode(strip, ordered, dec_gain, kv_weight, head_weight, head_count)
    isobar_pieces = lax.map(decode_block, out_blocks)
    predicted_tiles = isobar_pieces.transpose(1, 2, 0, 3).reshape(ISOBAR_NUMBER, MERIDIAN_TILES, ZONAL_TILES * TILE_ENTRIES)
    return (hidden_state_out, predicted_tiles)
```

```python
import functools
import math

import jax
import jax.numpy as jnp
import numpy as np
from jax import lax
from jax.experimental import pallas as pl
from jax.experimental.pallas import tpu as pltpu
from jax.sharding import PartitionSpec as P

EPSILON = 1e-05
WIDTH = 512
HEADS = 16
HEAD_DIM = WIDTH // HEADS
TOKENS = 144
OWN = 288
TILE = 80
ROW = 24 * TILE
LOG2E = math.log2(math.e)
BF16 = jnp.bfloat16
F32 = jnp.float32


def dot_nn(a, b):
    return lax.dot_general(a, b, (((1,), (0,)), ((), ())), preferred_element_type=F32)


def dot_nt(a, b):
    return lax.dot_general(a, b, (((1,), (1,)), ((), ())), preferred_element_type=F32)


def split(value):
    high = value.astype(BF16)
    return high, (value - high.astype(F32)).astype(BF16)


def coordinate(steps):
    return np.sign(steps) * np.log2(np.abs(steps) + 1.0) / 3.0


def constants():
    place = np.arange(256)
    row, col = place // 23, place % 23
    inside = place < 253
    coords = np.zeros((256, 2), np.float32)
    coords[:, 0] = np.where(inside, coordinate((5 - row) * 8.0 / 5.0), 0.0)
    coords[:, 1] = np.where(inside, coordinate((11 - col) * 8.0 / 11.0), 0.0)
    compact = np.zeros((256, 256), np.float32)
    for part in range(2):
        for k in range(10):
            for x in range(12):
                compact[(k + 1 - part) * 23 + x, part * 128 + 12 * k + x] = 1.0
    index = np.zeros((OWN, 8), np.int32)
    cell = np.arange(OWN)
    block, rest = cell // TOKENS, cell % TOKENS
    index[:, 0] = rest // 12 * 24
    index[:, 1] = block * 12 + rest % 12
    index[:, 2] = cell // 24 * 12
    index[:, 3] = cell % 24
    index[:, 4] = rest % 12
    slot, lat = cell // 24, cell % 24
    index[:48, 5] = (lat // 6 * 16 + slot * 6 + lat % 6)[:48]
    return coords, compact.astype(BF16), index


def norm(values):
    centre = values - jnp.mean(values, axis=-1, keepdims=True)
    spread = jnp.mean(centre * centre, axis=-1, keepdims=True)
    return centre * lax.rsqrt(spread + EPSILON)


def kernel(
    lon_count,
    lev_count,
    offset_ref,
    order_ref,
    latents_hbm,
    wqkv_hbm,
    wproj_hbm,
    wkv_hbm,
    post_gain_ref,
    first_ref,
    first_offset_ref,
    second_ref,
    dec_gain_ref,
    head_ref,
    queries_ref,
    coords_ref,
    compact_ref,
    index_ref,
    hidden_ref,
    tiles_ref,
    own_ref,
    wqkv_ref,
    wproj_ref,
    wkv_ref,
    turned_ref,
    halo_ref,
    shifted_ref,
    lattice_ref,
    packed_ref,
    packed_halo_ref,
    attended_ref,
    level_query_ref,
    result_ref,
    send_ref,
    receive_ref,
    local_sem,
    halo_send_sem,
    halo_receive_sem,
    tile_send_sem,
    tile_receive_sem,
):
    lon = lax.axis_index("lon")
    lev = lax.axis_index("lev")
    west = lax.rem(lon + lon_count - 1, lon_count)
    east = lax.rem(lon + 1, lon_count)
    mesh_id = pl.DeviceIdType.MESH

    barrier = pltpu.get_barrier_semaphore()
    for side in (west, east):
        pl.semaphore_signal(barrier, inc=1, device_id=(side, lev), device_id_type=mesh_id)
    for step in range(1, lev_count):
        pl.semaphore_signal(
            barrier,
            inc=1,
            device_id=(lon, lax.rem(lev + step, lev_count)),
            device_id_type=mesh_id,
        )

    loads = []
    for place, (source, target) in enumerate(
        (
            (latents_hbm, own_ref),
            (wqkv_hbm, wqkv_ref),
            (wproj_hbm, wproj_ref),
            (wkv_hbm, wkv_ref),
        )
    ):
        load = pltpu.make_async_copy(source, target, local_sem.at[place])
        load.start()
        loads.append(load)

    offset = offset_ref[0]

    turned_col = index_ref[:, 1:2] + offset
    turned_col = index_ref[:, 0:1] + jnp.where(turned_col >= 24, turned_col - 24, turned_col)
    cells = lax.broadcasted_iota(jnp.int32, (OWN, OWN), 1)
    turn = jnp.where(cells == turned_col, 1.0, 0.0).astype(BF16)
    loads[0].wait()
    turned_ref[...] = dot_nn(turn, own_ref[...]).astype(BF16)

    pl.semaphore_wait(barrier, 2 + lev_count - 1)
    halo_copies = []
    for place, side in enumerate((east, west)):
        copy = pltpu.make_async_remote_copy(
            src_ref=turned_ref.at[pl.ds(TOKENS, TOKENS)],
            dst_ref=halo_ref.at[place],
            send_sem=halo_send_sem.at[place],
            recv_sem=halo_receive_sem.at[place],
            device_id=(side, lev),
            device_id_type=mesh_id,
        )
        copy.start()
        halo_copies.append(copy)

    second_high, second_low = split(jnp.transpose(second_ref[...]))
    second_both = jnp.concatenate([second_high, second_low], axis=0)
    flat_part = (
        coords_ref[:, 0:1] * first_ref[1:2, :]
        + coords_ref[:, 1:2] * first_ref[2:3, :]
        + first_offset_ref[...]
    )
    for a in range(3):
        depth_coord = float(coordinate(np.float64((1 - a) * 8.0)))
        hidden = jnp.maximum(flat_part + depth_coord * first_ref[0:1, :], 0.0)
        hidden_high, hidden_low = split(hidden)
        both = dot_nt(second_both, hidden_high)
        logits = both[:HEADS] + both[HEADS:] + dot_nt(second_high, hidden_low)
        table = (16.0 * LOG2E) / (1.0 + jnp.exp(-logits))
        for x in range(12):
            rolled = table if x == 11 else pltpu.roll(table, 256 - (11 - x), 1)
            high, low = split(rolled)
            shifted_ref[pl.ds(x * HEADS, HEADS), :] = high
            shifted_ref[pl.ds((12 + x) * HEADS, HEADS), :] = low
        spread_out = dot_nn(shifted_ref[...], compact_ref[...])
        spread_out = spread_out[:192] + spread_out[192:]
        lattice_ref[a, pl.ds(0, 192), :] = spread_out[:, :128]
        lattice_ref[a, pl.ds(192, 192), :] = spread_out[:, 128:]

    loads[1].wait()
    turned = turned_ref[...]
    scale = LOG2E / math.sqrt(HEAD_DIM)
    packed_ref[:, :WIDTH] = (dot_nn(turned, wqkv_ref[:, :WIDTH]) * scale).astype(BF16)
    packed_ref[:, WIDTH:] = dot_nn(turned, wqkv_ref[:, WIDTH:]).astype(BF16)

    for copy in halo_copies:
        copy.wait()
    upper = index_ref[:TOKENS, 4:5] >= 12 - offset
    halo = jnp.where(upper, halo_ref[1].astype(F32), halo_ref[0].astype(F32)).astype(BF16)
    packed_halo_ref[...] = dot_nn(halo, wqkv_ref[:, WIDTH:]).astype(BF16)

    lane256 = lax.broadcasted_iota(jnp.int32, (TOKENS, 256), 1)
    lane128 = lax.broadcasted_iota(jnp.int32, (24, 128), 1)
    edge = pl.ds(TOKENS, TOKENS)
    zero = jnp.zeros((), BF16)
    for half in range(2):
        lanes = pl.ds(256 * half, 256)
        q_inner = packed_ref[pl.ds(0, TOKENS), lanes]
        k_inner = packed_ref[pl.ds(0, TOKENS), pl.ds(WIDTH + 256 * half, 256)]
        v_inner = packed_ref[pl.ds(0, TOKENS), pl.ds(2 * WIDTH + 256 * half, 256)]
        q_edge = packed_ref[edge, lanes]
        k_edge = packed_ref[edge, pl.ds(WIDTH + 256 * half, 256)].astype(F32)
        v_edge = packed_ref[edge, pl.ds(2 * WIDTH + 256 * half, 256)].astype(F32)
        k_halo = packed_halo_ref[:, lanes].astype(F32)
        v_halo = packed_halo_ref[:, pl.ds(WIDTH + 256 * half, 256)].astype(F32)
        k_upper = jnp.where(upper, k_edge, k_halo).astype(BF16)
        k_lower = jnp.where(upper, k_halo, k_edge).astype(BF16)
        v_upper = jnp.where(upper, v_edge, v_halo).astype(BF16)
        v_lower = jnp.where(upper, v_halo, v_edge).astype(BF16)
        q_upper = jnp.where(upper, q_edge.astype(F32), 0.0).astype(BF16)
        q_lower = jnp.where(upper, 0.0, q_edge.astype(F32)).astype(BF16)
        out_inner = jnp.zeros((TOKENS, 256), F32)
        out_upper = jnp.zeros((TOKENS, 256), F32)
        out_lower = jnp.zeros((TOKENS, 256), F32)
        for local_head in range(8):
            h = 8 * half + local_head
            mine = lane256 // HEAD_DIM == local_head
            lattice = [lattice_ref[a, pl.ds(h, 24, stride=HEADS), :] for a in range(3)]
            pieces = []
            for dz in range(2):
                for m in range(3):
                    start = (4 - 2 * m) * 12
                    near = lattice[1 - dz]
                    if start:
                        near = pltpu.roll(near, 128 - start, 1)
                    far = pltpu.roll(lattice[2 - dz], 72 - start, 1)
                    pieces.append(
                        jnp.concatenate([jnp.where(lane128 < 72, near, far), far[:, :16]], axis=1)
                    )
            bias = jnp.concatenate(pieces, axis=0)

            def soft(scores):
                raised = jnp.exp2(scores - jnp.max(scores, axis=-1, keepdims=True))
                total = jnp.sum(raised, axis=-1, keepdims=True)
                return (raised * (1.0 / total)).astype(BF16)

            weights = soft(dot_nt(jnp.where(mine, q_inner, zero), k_inner) + bias)
            out_inner = jnp.where(mine, dot_nn(weights, v_inner), out_inner)
            weights = soft(
                dot_nt(jnp.where(mine, q_upper, zero), k_upper)
                + dot_nt(jnp.where(mine, q_lower, zero), k_lower)
                + bias
            )
            out_upper = jnp.where(mine, dot_nn(weights, v_upper), out_upper)
            out_lower = jnp.where(mine, dot_nn(weights, v_lower), out_lower)
        attended_ref[pl.ds(0, TOKENS), lanes] = out_inner.astype(BF16)
        attended_ref[edge, lanes] = jnp.where(upper, out_upper, out_lower).astype(BF16)

    loads[2].wait()
    projected = dot_nn(attended_ref[...], wproj_ref[...])
    mixed = (turned_ref[...].astype(F32) + post_gain_ref[...] * norm(projected)).astype(BF16)
    back_col = index_ref[:, 3:4] - offset
    back_col = jnp.where(back_col < 0, back_col + 24, back_col)
    back_col = index_ref[:, 2:3] + jnp.where(back_col >= 12, back_col + (TOKENS - 12), back_col)
    turn_back = jnp.where(cells == back_col, 1.0, 0.0).astype(BF16)
    state = dot_nn(turn_back, mixed)
    hidden_ref[...] = state.astype(BF16)

    normed = (dec_gain_ref[...] * norm(state)).astype(BF16)
    loads[3].wait()
    keys = dot_nn(normed, wkv_ref[:, :WIDTH]).astype(BF16)
    values = dot_nn(normed, wkv_ref[:, WIDTH:]).astype(BF16).astype(F32)
    head_lane = lax.broadcasted_iota(jnp.int32, (HEADS, WIDTH), 1) // HEAD_DIM
    head_row = lax.broadcasted_iota(jnp.int32, (HEADS, WIDTH), 0)
    for i in range(8):
        query = queries_ref[pl.ds(order_ref[i], 1), :]
        level_query_ref[pl.ds(i * HEADS, HEADS), :] = jnp.where(
            head_lane == head_row, query, 0.0
        ).astype(BF16)
    scores = dot_nt(keys, level_query_ref[...]) * (0.5 / math.sqrt(HEAD_DIM))
    upper_weight = 0.5 + 0.5 * jnp.tanh(scores[:TOKENS] - scores[TOKENS:])
    weight_high, weight_low = split(upper_weight)
    weight_both = jnp.concatenate([weight_high, weight_low], axis=1)
    expand = jnp.where(
        lax.broadcasted_iota(jnp.int32, (256, WIDTH), 0) % HEADS
        == lax.broadcasted_iota(jnp.int32, (256, WIDTH), 1) // HEAD_DIM,
        1.0,
        0.0,
    ).astype(BF16)
    level_lane = lane256 % 128 // HEADS
    value_lower = values[TOKENS:]
    value_step = values[:TOKENS] - value_lower
    result_ref[pl.ds(8 * TOKENS, 96), :] = jnp.zeros((96, 128), F32)
    for i in range(8):
        wide = dot_nn(jnp.where(level_lane == i, weight_both, zero), expand)
        decoded = (value_lower + wide * value_step).astype(BF16)
        result_ref[pl.ds(i * TOKENS, TOKENS), :TILE] = dot_nn(decoded, head_ref[...])
    lane16 = lax.broadcasted_iota(jnp.int32, (16, 128), 1)
    for target in range(lev_count):
        turned_tiles = []
        for x in range(24):
            slab = result_ref[pl.ds(target * 2 * TOKENS + x, 16, stride=24), :]
            turned_tiles.append(pltpu.roll(slab, x * TILE % 128, 1) if x * TILE % 128 else slab)
        for k in range(ROW // 128):
            first = 128 * k // TILE
            tile = turned_tiles[first]
            for x in range(first + 1, (128 * k + 127) // TILE + 1):
                tile = jnp.where(lane16 >= TILE * x - 128 * k, turned_tiles[x], tile)
            send_ref[target, :, pl.ds(128 * k, 128)] = tile.astype(BF16)

    tile_copies = []
    for step in range(1, lev_count):
        target = lax.rem(lev + step, lev_count)
        copy = pltpu.make_async_remote_copy(
            src_ref=send_ref.at[target],
            dst_ref=receive_ref.at[lev],
            send_sem=tile_send_sem.at[step - 1],
            recv_sem=tile_receive_sem.at[step - 1],
            device_id=(lon, target),
            device_id_type=mesh_id,
        )
        copy.start()
        tile_copies.append(copy)
    receive_ref[pl.ds(lev, 1)] = send_ref[pl.ds(lev, 1)]
    for copy in tile_copies:
        copy.wait()
    gather = jnp.where(
        lax.broadcasted_iota(jnp.int32, (48, 16 * lev_count), 1) == index_ref[:48, 5:6], 1.0, 0.0
    ).astype(BF16)
    received = receive_ref[...].reshape(16 * lev_count, ROW)
    tiles_ref[...] = dot_nn(gather, received).astype(BF16)


def body(
    latents,
    shift_offset,
    qkv_weight,
    proj_weight,
    post_gain,
    bias_first_weight,
    bias_first_offset,
    bias_second_weight,
    dec_gain,
    kv_weight,
    head_weight,
    level_queries,
    level_order,
):
    lon_count = lax.axis_size("lon")
    lev_count = lax.axis_size("lev")
    coords, compact, index = constants()
    smem = pl.BlockSpec(memory_space=pltpu.SMEM)
    vmem = pl.BlockSpec(memory_space=pltpu.VMEM)
    anywhere = pl.BlockSpec(memory_space=pl.ANY)
    dma = pltpu.SemaphoreType.DMA
    hidden, tiles = pl.pallas_call(
        functools.partial(kernel, lon_count, lev_count),
        out_shape=(
            jax.ShapeDtypeStruct((OWN, WIDTH), BF16),
            jax.ShapeDtypeStruct((48, ROW), BF16),
        ),
        in_specs=[smem, smem] + [anywhere] * 4 + [vmem] * 10,
        out_specs=(vmem, vmem),
        scratch_shapes=[
            pltpu.VMEM((OWN, WIDTH), BF16),
            pltpu.VMEM((WIDTH, 3 * WIDTH), BF16),
            pltpu.VMEM((WIDTH, WIDTH), BF16),
            pltpu.VMEM((WIDTH, 2 * WIDTH), BF16),
            pltpu.VMEM((OWN, WIDTH), BF16),
            pltpu.VMEM((2, TOKENS, WIDTH), BF16),
            pltpu.VMEM((384, 256), BF16),
            pltpu.VMEM((3, 384, 128), F32),
            pltpu.VMEM((OWN, 3 * WIDTH), BF16),
            pltpu.VMEM((TOKENS, 2 * WIDTH), BF16),
            pltpu.VMEM((OWN, WIDTH), BF16),
            pltpu.VMEM((128, WIDTH), BF16),
            pltpu.VMEM((8 * TOKENS + 96, 128), F32),
            pltpu.VMEM((lev_count, 16, ROW), BF16),
            pltpu.VMEM((lev_count, 16, ROW), BF16),
            dma((4,)),
            dma((2,)),
            dma((2,)),
            dma((lev_count - 1,)),
            dma((lev_count - 1,)),
        ],
        compiler_params=pltpu.CompilerParams(
            collective_id=0, has_side_effects=True, vmem_limit_bytes=40 * 1024 * 1024
        ),
    )(
        shift_offset,
        level_order,
        latents.reshape(OWN, WIDTH),
        qkv_weight,
        proj_weight,
        kv_weight,
        post_gain.reshape(1, WIDTH),
        bias_first_weight,
        bias_first_offset.reshape(1, WIDTH),
        bias_second_weight,
        dec_gain.reshape(1, WIDTH),
        head_weight,
        level_queries,
        jnp.asarray(coords),
        jnp.asarray(compact),
        jnp.asarray(index),
    )
    return hidden.reshape(latents.shape), tiles.reshape(2, 24, ROW)


def solution(mesh):
    return jax.shard_map(
        body,
        mesh=mesh,
        in_specs=(P(None, "lev", "lon", None),) + (P(),) * 12,
        out_specs=(P(None, "lev", "lon", None), P("lev", None, "lon")),
        check_vma=False,
    )
```

```python
import functools
import math

import jax
import jax.numpy as jnp
import numpy as np
from jax import lax
from jax.experimental import pallas as pl
from jax.experimental.pallas import tpu as pltpu
from jax.sharding import PartitionSpec as P

EPSILON = 1e-05
WIDTH = 512
HEADS = 16
HEAD_DIM = WIDTH // HEADS
TOKENS = 144
OWN = 288
TILE = 80
ROW = 24 * TILE
LOG2E = math.log2(math.e)
BF16 = jnp.bfloat16
F32 = jnp.float32


def dot_nn(a, b):
    return lax.dot_general(a, b, (((1,), (0,)), ((), ())), preferred_element_type=F32)


def dot_nt(a, b):
    return lax.dot_general(a, b, (((1,), (1,)), ((), ())), preferred_element_type=F32)


def split(value):
    high = value.astype(BF16)
    return high, (value - high.astype(F32)).astype(BF16)


def coordinate(steps):
    return np.sign(steps) * np.log2(np.abs(steps) + 1.0) / 3.0


def constants():
    place = np.arange(256)
    row, col = place // 23, place % 23
    inside = place < 253
    coords = np.zeros((256, 2), np.float32)
    coords[:, 0] = np.where(inside, coordinate((5 - row) * 8.0 / 5.0), 0.0)
    coords[:, 1] = np.where(inside, coordinate((11 - col) * 8.0 / 11.0), 0.0)
    compact = np.zeros((256, 256), np.float32)
    for part in range(2):
        for k in range(10):
            for x in range(12):
                compact[(k + 1 - part) * 23 + x, part * 128 + 12 * k + x] = 1.0
    index = np.zeros((OWN, 8), np.int32)
    cell = np.arange(OWN)
    block, rest = cell // TOKENS, cell % TOKENS
    index[:, 0] = rest // 12 * 24
    index[:, 1] = block * 12 + rest % 12
    index[:, 2] = cell // 24 * 12
    index[:, 3] = cell % 24
    index[:, 4] = rest % 12
    slot, lat = cell // 24, cell % 24
    index[:48, 5] = (lat // 6 * 48 + slot * 24 + lat % 6 * 4)[:48]
    return coords, compact.astype(BF16), index


def norm(values):
    centre = values - jnp.mean(values, axis=-1, keepdims=True)
    spread = jnp.mean(centre * centre, axis=-1, keepdims=True)
    return centre * lax.rsqrt(spread + EPSILON)


def kernel(
    lon_count,
    lev_count,
    offset_hbm,
    order_hbm,
    latents_hbm,
    wqkv_hbm,
    wproj_hbm,
    wkv_hbm,
    post_gain_hbm,
    first_hbm,
    first_offset_hbm,
    second_hbm,
    dec_gain_hbm,
    head_hbm,
    queries_hbm,
    coords_hbm,
    compact_hbm,
    index_hbm,
    hidden_ref,
    tiles_ref,
    offset_ref,
    order_ref,
    own_ref,
    wqkv_ref,
    wproj_ref,
    wkv_ref,
    post_gain_ref,
    first_ref,
    first_offset_ref,
    second_ref,
    dec_gain_ref,
    head_ref,
    queries_ref,
    coords_ref,
    compact_ref,
    index_ref,
    turned_ref,
    halo_ref,
    shifted_ref,
    lattice_ref,
    bias_ref,
    packed_ref,
    packed_halo_ref,
    attended_ref,
    level_query_ref,
    result_ref,
    send_ref,
    receive_ref,
    local_sem,
    halo_send_sem,
    halo_receive_sem,
    tile_send_sem,
    tile_receive_sem,
):
    lon = lax.axis_index("lon")
    lev = lax.axis_index("lev")
    west = lax.rem(lon + lon_count - 1, lon_count)
    east = lax.rem(lon + 1, lon_count)
    mesh_id = pl.DeviceIdType.MESH

    barrier = pltpu.get_barrier_semaphore()
    for side in (west, east):
        pl.semaphore_signal(barrier, inc=1, device_id=(side, lev), device_id_type=mesh_id)
    for step in range(1, lev_count):
        pl.semaphore_signal(
            barrier,
            inc=1,
            device_id=(lon, lax.rem(lev + step, lev_count)),
            device_id_type=mesh_id,
        )

    loads = {}
    for place, (name, source, target) in enumerate(
        (
            ("index", index_hbm, index_ref),
            ("offset", offset_hbm, offset_ref),
            ("latents", latents_hbm, own_ref),
            ("coords", coords_hbm, coords_ref),
            ("first", first_hbm, first_ref),
            ("first_offset", first_offset_hbm, first_offset_ref),
            ("second", second_hbm, second_ref),
            ("compact", compact_hbm, compact_ref),
            ("wqkv", wqkv_hbm, wqkv_ref),
            ("wproj", wproj_hbm, wproj_ref),
            ("post_gain", post_gain_hbm, post_gain_ref),
            ("dec_gain", dec_gain_hbm, dec_gain_ref),
            ("wkv", wkv_hbm, wkv_ref),
            ("order", order_hbm, order_ref),
            ("queries", queries_hbm, queries_ref),
            ("head", head_hbm, head_ref.at[pl.ds(0, TILE)]),
        )
    ):
        loads[name] = pltpu.make_async_copy(source, target, local_sem.at[place])
        loads[name].start()

    def loaded(*names):
        for name in names:
            loads[name].wait()

    loaded("index", "offset")
    offset = offset_ref[0]
    head_ref[pl.ds(TILE, 128 - TILE), :] = jnp.zeros((128 - TILE, WIDTH), BF16)

    turned_col = index_ref[:, 1:2] + offset
    turned_col = index_ref[:, 0:1] + jnp.where(turned_col >= 24, turned_col - 24, turned_col)
    cells = lax.broadcasted_iota(jnp.int32, (OWN, OWN), 1)
    turn = jnp.where(cells == turned_col, 1.0, 0.0).astype(BF16)
    loaded("latents")
    turned_ref[...] = dot_nn(turn, own_ref[...]).astype(BF16)

    pl.semaphore_wait(barrier, 2 + lev_count - 1)
    halo_copies = []
    for place, side in enumerate((east, west)):
        copy = pltpu.make_async_remote_copy(
            src_ref=turned_ref.at[pl.ds(TOKENS, TOKENS)],
            dst_ref=halo_ref.at[place],
            send_sem=halo_send_sem.at[place],
            recv_sem=halo_receive_sem.at[place],
            device_id=(side, lev),
            device_id_type=mesh_id,
        )
        copy.start()
        halo_copies.append(copy)

    lane24 = lax.broadcasted_iota(jnp.int32, (24, 128), 1)
    loaded("coords", "first", "first_offset", "second", "compact")
    second_high, second_low = split(second_ref[...])
    second_both = jnp.concatenate([second_high, second_low], axis=0)
    flat_part = (
        coords_ref[:, 0:1] * first_ref[1:2, :]
        + coords_ref[:, 1:2] * first_ref[2:3, :]
        + first_offset_ref[...]
    )
    for a in range(3):
        depth_coord = float(coordinate(np.float64((1 - a) * 8.0)))
        hidden = jnp.maximum(flat_part + depth_coord * first_ref[0:1, :], 0.0)
        hidden_high, hidden_low = split(hidden)
        both = dot_nt(second_both, hidden_high)
        logits = both[:HEADS] + both[HEADS:] + dot_nt(second_high, hidden_low)
        table = (16.0 * LOG2E) / (1.0 + jnp.exp(-logits))
        for x in range(12):
            rolled = table if x == 11 else pltpu.roll(table, 256 - (11 - x), 1)
            high, low = split(rolled)
            shifted_ref[pl.ds(x * HEADS, HEADS), :] = high
            shifted_ref[pl.ds((12 + x) * HEADS, HEADS), :] = low
        spread_out = dot_nn(shifted_ref[...], compact_ref[...])
        spread_out = spread_out[:192] + spread_out[192:]
        lattice_ref[a, pl.ds(0, 192), :] = spread_out[:, :128]
        lattice_ref[a, pl.ds(192, 192), :] = spread_out[:, 128:]

    for h in range(HEADS):
        lattice = [lattice_ref[a, pl.ds(h, 24, stride=HEADS), :] for a in range(3)]
        for dz in range(2):
            for m in range(3):
                start = (4 - 2 * m) * 12
                rows = pl.ds(72 * dz + 24 * m, 24)
                near = lattice[1 - dz]
                if start:
                    near = pltpu.roll(near, 128 - start, 1)
                far = pltpu.roll(lattice[2 - dz], 72 - start, 1)
                bias_ref[h, rows, :128] = jnp.where(lane24 < 72, near, far)
                bias_ref[h, rows, 128:] = far[:, :16]

    loaded("wqkv")
    turned = turned_ref[...]
    scale = LOG2E / math.sqrt(HEAD_DIM)
    packed_ref[:, :WIDTH] = (dot_nn(turned, wqkv_ref[:, :WIDTH]) * scale).astype(BF16)
    packed_ref[:, WIDTH:] = dot_nn(turned, wqkv_ref[:, WIDTH:]).astype(BF16)

    def soft(scores):
        raised = jnp.exp2(scores - jnp.max(scores, axis=-1, keepdims=True))
        total = jnp.sum(raised, axis=-1, keepdims=True)
        return (raised * pl.reciprocal(total, approx=True)).astype(BF16)

    lane128 = lax.broadcasted_iota(jnp.int32, (TOKENS, 128), 1)
    inner = pl.ds(0, TOKENS)
    zero = jnp.zeros((), BF16)
    for quad in range(4):
        q_inner = packed_ref[inner, pl.ds(128 * quad, 128)]
        k_inner = packed_ref[inner, pl.ds(WIDTH + 128 * quad, 128)]
        v_inner = packed_ref[inner, pl.ds(2 * WIDTH + 128 * quad, 128)]
        out = jnp.zeros((TOKENS, 128), F32)
        for j in range(4):
            mine = lane128 // HEAD_DIM == j
            weights = soft(dot_nt(jnp.where(mine, q_inner, zero), k_inner) + bias_ref[4 * quad + j])
            out = jnp.where(mine, dot_nn(weights, v_inner), out)
        attended_ref[inner, pl.ds(128 * quad, 128)] = out.astype(BF16)

    for copy in halo_copies:
        copy.wait()
    upper = index_ref[:TOKENS, 4:5] >= 12 - offset
    halo = jnp.where(upper, halo_ref[1].astype(F32), halo_ref[0].astype(F32)).astype(BF16)
    packed_halo_ref[...] = dot_nn(halo, wqkv_ref[:, WIDTH:]).astype(BF16)
    lane256 = lax.broadcasted_iota(jnp.int32, (TOKENS, 256), 1)
    edge = pl.ds(TOKENS, TOKENS)
    for quad in range(4):
        q_edge = packed_ref[edge, pl.ds(128 * quad, 128)].astype(F32)
        k_edge = packed_ref[edge, pl.ds(WIDTH + 128 * quad, 128)].astype(F32)
        v_edge = packed_ref[edge, pl.ds(2 * WIDTH + 128 * quad, 128)].astype(F32)
        k_halo = packed_halo_ref[:, pl.ds(128 * quad, 128)].astype(F32)
        v_halo = packed_halo_ref[:, pl.ds(WIDTH + 128 * quad, 128)].astype(F32)
        q_both = jnp.concatenate([jnp.where(upper, q_edge, 0.0), jnp.where(upper, 0.0, q_edge)], 1)
        k_both = jnp.concatenate(
            [jnp.where(upper, k_edge, k_halo), jnp.where(upper, k_halo, k_edge)], 1
        )
        v_both = jnp.concatenate(
            [jnp.where(upper, v_edge, v_halo), jnp.where(upper, v_halo, v_edge)], 1
        )
        q_both, k_both, v_both = q_both.astype(BF16), k_both.astype(BF16), v_both.astype(BF16)
        out_upper = jnp.zeros((TOKENS, 128), F32)
        out_lower = jnp.zeros((TOKENS, 128), F32)
        for j in range(4):
            mine = lane256 % 128 // HEAD_DIM == j
            weights = soft(dot_nt(jnp.where(mine, q_both, zero), k_both) + bias_ref[4 * quad + j])
            both = dot_nn(weights, v_both)
            mine = lane128 // HEAD_DIM == j
            out_upper = jnp.where(mine, both[:, :128], out_upper)
            out_lower = jnp.where(mine, both[:, 128:], out_lower)
        out = jnp.where(upper, out_upper, out_lower)
        attended_ref[edge, pl.ds(128 * quad, 128)] = out.astype(BF16)

    loaded("wproj", "post_gain", "dec_gain")
    projected = dot_nn(attended_ref[...], wproj_ref[...])
    mixed = (turned_ref[...].astype(F32) + post_gain_ref[...] * norm(projected)).astype(BF16)
    back_col = index_ref[:, 3:4] - offset
    back_col = jnp.where(back_col < 0, back_col + 24, back_col)
    back_col = index_ref[:, 2:3] + jnp.where(back_col >= 12, back_col + (TOKENS - 12), back_col)
    turn_back = jnp.where(cells == back_col, 1.0, 0.0).astype(BF16)
    state = dot_nn(turn_back, mixed)
    hidden_ref[...] = state.astype(BF16)

    normed = (dec_gain_ref[...] * norm(state)).astype(BF16)
    loaded("wkv", "order", "queries", "head")
    keys = dot_nn(normed, wkv_ref[:, :WIDTH]).astype(BF16)
    values = dot_nn(normed, wkv_ref[:, WIDTH:]).astype(BF16).astype(F32)
    head_lane = lax.broadcasted_iota(jnp.int32, (HEADS, WIDTH), 1) // HEAD_DIM
    head_row = lax.broadcasted_iota(jnp.int32, (HEADS, WIDTH), 0)
    for i in range(8):
        query = queries_ref[pl.ds(order_ref[i], 1), :]
        level_query_ref[pl.ds(i * HEADS, HEADS), :] = jnp.where(
            head_lane == head_row, query, 0.0
        ).astype(BF16)
    scores = dot_nt(keys, level_query_ref[...]) * (0.5 / math.sqrt(HEAD_DIM))
    upper_weight = 0.5 + 0.5 * jnp.tanh(scores[:TOKENS] - scores[TOKENS:])
    weight_high, weight_low = split(upper_weight)
    weight_both = jnp.concatenate([weight_high, weight_low], axis=1)
    expand = jnp.where(
        lax.broadcasted_iota(jnp.int32, (256, WIDTH), 0) % HEADS
        == lax.broadcasted_iota(jnp.int32, (256, WIDTH), 1) // HEAD_DIM,
        1.0,
        0.0,
    ).astype(BF16)
    level_lane = lane256 % 128 // HEADS
    value_lower = values[TOKENS:]
    value_step = values[:TOKENS] - value_lower
    lane48 = lax.broadcasted_iota(jnp.int32, (48, 128), 1)

    def piece(parts):
        tile = parts[0][1]
        for start, part in parts[1:]:
            tile = jnp.where(lane48 >= start, part, tile)
        return tile

    tile_copies = []
    for step in (2, 3, 1, 0):
        target = lax.rem(lev + step, lev_count)
        for j in range(2):
            wide = dot_nn(jnp.where(level_lane == 2 * target + j, weight_both, zero), expand)
            decoded = (value_lower + wide * value_step).astype(BF16)
            result_ref[step, pl.ds(j * TOKENS, TOKENS), :] = dot_nt(decoded, head_ref[...])
        slabs = []
        for x in range(6):
            slab = result_ref[step, pl.ds(x, 48, stride=6), :]
            slabs.append(pltpu.roll(slab, x * TILE % 128, 1) if x * TILE % 128 else slab)
        block = jnp.concatenate(
            [
                piece([(TILE * x - 128 * k, slabs[x]) for x in range(128 * k // TILE, min((128 * k + 127) // TILE, 5) + 1)])
                for k in range(4)
            ],
            axis=1,
        ).astype(BF16)
        if step == 0:
            receive_ref[pl.ds(lev, 1)] = block[None]
            continue
        send_ref[step - 1] = block
        copy = pltpu.make_async_remote_copy(
            src_ref=send_ref.at[step - 1],
            dst_ref=receive_ref.at[lev],
            send_sem=tile_send_sem.at[step - 1],
            recv_sem=tile_receive_sem.at[step - 1],
            device_id=(lon, target),
            device_id_type=mesh_id,
        )
        copy.start()
        tile_copies.append(copy)

    rows = 48 * lev_count
    place = lax.broadcasted_iota(jnp.int32, (48, rows), 1) - index_ref[:48, 5:6]
    gather = jnp.concatenate([jnp.where(place == q, 1.0, 0.0) for q in range(4)], 0).astype(BF16)
    for copy in tile_copies:
        copy.wait()
    sorted_rows = dot_nn(gather, receive_ref[...].reshape(rows, WIDTH))
    parts = [[] for _ in range(ROW // 128)]
    for q in range(4):
        for c in range(4):
            part = sorted_rows[48 * q : 48 * q + 48, 128 * c : 128 * c + 128]
            if 480 * q % 128:
                part = pltpu.roll(part, 480 * q % 128, 1)
            first = 480 * q + 128 * c
            last = min(first + 128, 480 * q + 480) - 1
            for k in range(first // 128, last // 128 + 1):
                parts[k].append((first - 128 * k, part))
    for k in range(ROW // 128):
        tiles_ref[:, pl.ds(128 * k, 128)] = piece(parts[k]).astype(BF16)


def body(
    latents,
    shift_offset,
    qkv_weight,
    proj_weight,
    post_gain,
    bias_first_weight,
    bias_first_offset,
    bias_second_weight,
    dec_gain,
    kv_weight,
    head_weight,
    level_queries,
    level_order,
):
    lon_count = lax.axis_size("lon")
    lev_count = lax.axis_size("lev")
    coords, compact, index = constants()
    vmem = pl.BlockSpec(memory_space=pltpu.VMEM)
    hbm = pl.BlockSpec(memory_space=pltpu.HBM)
    dma = pltpu.SemaphoreType.DMA
    hidden, tiles = pl.pallas_call(
        functools.partial(kernel, lon_count, lev_count),
        out_shape=(
            jax.ShapeDtypeStruct((OWN, WIDTH), BF16),
            jax.ShapeDtypeStruct((48, ROW), BF16),
        ),
        in_specs=[hbm] * 16,
        out_specs=(vmem, vmem),
        scratch_shapes=[
            pltpu.SMEM((1,), jnp.int32),
            pltpu.SMEM((8,), jnp.int32),
            pltpu.VMEM((OWN, WIDTH), BF16),
            pltpu.VMEM((WIDTH, 3 * WIDTH), BF16),
            pltpu.VMEM((WIDTH, WIDTH), BF16),
            pltpu.VMEM((WIDTH, 2 * WIDTH), BF16),
            pltpu.VMEM((1, WIDTH), F32),
            pltpu.VMEM((3, WIDTH), F32),
            pltpu.VMEM((1, WIDTH), F32),
            pltpu.VMEM((HEADS, WIDTH), F32),
            pltpu.VMEM((1, WIDTH), F32),
            pltpu.VMEM((128, WIDTH), BF16),
            pltpu.VMEM((8, WIDTH), F32),
            pltpu.VMEM((256, 2), F32),
            pltpu.VMEM((256, 256), BF16),
            pltpu.VMEM((OWN, 8), jnp.int32),
            pltpu.VMEM((OWN, WIDTH), BF16),
            pltpu.VMEM((2, TOKENS, WIDTH), BF16),
            pltpu.VMEM((384, 256), BF16),
            pltpu.VMEM((3, 384, 128), F32),
            pltpu.VMEM((HEADS, TOKENS, TOKENS), F32),
            pltpu.VMEM((OWN, 3 * WIDTH), BF16),
            pltpu.VMEM((TOKENS, 2 * WIDTH), BF16),
            pltpu.VMEM((OWN, WIDTH), BF16),
            pltpu.VMEM((128, WIDTH), BF16),
            pltpu.VMEM((lev_count, 2 * TOKENS, 128), F32),
            pltpu.VMEM((lev_count - 1, 48, WIDTH), BF16),
            pltpu.VMEM((lev_count, 48, WIDTH), BF16),
            dma((16,)),
            dma((2,)),
            dma((2,)),
            dma((lev_count - 1,)),
            dma((lev_count - 1,)),
        ],
        compiler_params=pltpu.CompilerParams(
            collective_id=0, has_side_effects=True, vmem_limit_bytes=40 * 1024 * 1024
        ),
    )(
        shift_offset,
        *(
            pltpu.with_memory_space_constraint(value, pltpu.HBM)
            for value in (
                level_order,
                latents.reshape(OWN, WIDTH),
                qkv_weight,
                proj_weight,
                kv_weight,
                post_gain.reshape(1, WIDTH),
                bias_first_weight,
                bias_first_offset.reshape(1, WIDTH),
                bias_second_weight.T,
                dec_gain.reshape(1, WIDTH),
                head_weight.T,
                level_queries,
                jnp.asarray(coords),
                jnp.asarray(compact),
                jnp.asarray(index),
            )
        )
    )
    return hidden.reshape(latents.shape), tiles.reshape(2, 24, ROW)


def solution(mesh):
    return jax.shard_map(
        body,
        mesh=mesh,
        in_specs=(P(None, "lev", "lon", None),) + (P(),) * 12,
        out_specs=(P(None, "lev", "lon", None), P("lev", None, "lon")),
        check_vma=False,
    )
```

```python
import functools
import math

import jax
import jax.numpy as jnp
import numpy as np
from jax import lax
from jax.experimental import pallas as pl
from jax.experimental.pallas import tpu as pltpu
from jax.sharding import PartitionSpec as P

EPSILON = 1e-05
WIDTH = 512
HEADS = 16
HEAD_DIM = WIDTH // HEADS
TOKENS = 144
OWN = 288
TILE = 80
ROW = 24 * TILE
LOG2E = math.log2(math.e)
BF16 = jnp.bfloat16
F32 = jnp.float32


def dot_nn(a, b):
    return lax.dot_general(a, b, (((1,), (0,)), ((), ())), preferred_element_type=F32)


def dot_nt(a, b):
    return lax.dot_general(a, b, (((1,), (1,)), ((), ())), preferred_element_type=F32)


def split(value):
    high = value.astype(BF16)
    return high, (value - high.astype(F32)).astype(BF16)


def coordinate(steps):
    return np.sign(steps) * np.log2(np.abs(steps) + 1.0) / 3.0


def constants():
    place = np.arange(256)
    row, col = place // 23, place % 23
    inside = place < 253
    coords = np.zeros((256, 2), np.float32)
    coords[:, 0] = np.where(inside, coordinate((5 - row) * 8.0 / 5.0), 0.0)
    coords[:, 1] = np.where(inside, coordinate((11 - col) * 8.0 / 11.0), 0.0)
    compact = np.zeros((256, 256), np.float32)
    for part in range(2):
        for k in range(10):
            for x in range(12):
                compact[(k + 1 - part) * 23 + x, part * 128 + 12 * k + x] = 1.0
    return coords, compact.astype(BF16)


def over_twelve(value):
    return lax.shift_right_logical(value * 43691, 19)


def norm(values):
    centre = values - jnp.mean(values, axis=-1, keepdims=True)
    spread = jnp.mean(centre * centre, axis=-1, keepdims=True)
    return centre * lax.rsqrt(spread + EPSILON)


def kernel(
    lon_count,
    lev_count,
    offset_hbm,
    order_hbm,
    latents_hbm,
    wqkv_hbm,
    wproj_hbm,
    wkv_hbm,
    post_gain_hbm,
    first_hbm,
    first_offset_hbm,
    second_hbm,
    dec_gain_hbm,
    head_hbm,
    queries_hbm,
    coords_hbm,
    compact_hbm,
    hidden_ref,
    tiles_ref,
    offset_ref,
    order_ref,
    own_ref,
    wqkv_ref,
    wproj_ref,
    wkv_ref,
    post_gain_ref,
    first_ref,
    first_offset_ref,
    second_ref,
    dec_gain_ref,
    head_ref,
    queries_ref,
    coords_ref,
    compact_ref,
    turned_ref,
    halo_ref,
    shifted_ref,
    lattice_ref,
    bias_ref,
    packed_ref,
    packed_halo_ref,
    attended_ref,
    mixed_ref,
    level_query_ref,
    expand_ref,
    result_ref,
    send_ref,
    receive_ref,
    local_sem,
    halo_send_sem,
    halo_receive_sem,
    tile_send_sem,
    tile_receive_sem,
):
    lon = lax.axis_index("lon")
    lev = lax.axis_index("lev")
    west = lax.rem(lon + lon_count - 1, lon_count)
    east = lax.rem(lon + 1, lon_count)
    mesh_id = pl.DeviceIdType.MESH

    barrier = pltpu.get_barrier_semaphore()
    for side in (west, east):
        pl.semaphore_signal(barrier, inc=1, device_id=(side, lev), device_id_type=mesh_id)
    for step in range(1, lev_count):
        pl.semaphore_signal(
            barrier,
            inc=1,
            device_id=(lon, lax.rem(lev + step, lev_count)),
            device_id_type=mesh_id,
        )

    loads = {}
    for place, (name, source, target) in enumerate(
        (
            ("offset", offset_hbm, offset_ref),
            ("latents", latents_hbm, own_ref),
            ("coords", coords_hbm, coords_ref),
            ("first", first_hbm, first_ref),
            ("first_offset", first_offset_hbm, first_offset_ref),
            ("second", second_hbm, second_ref),
            ("compact", compact_hbm, compact_ref),
            ("wqkv", wqkv_hbm, wqkv_ref),
            ("wproj", wproj_hbm, wproj_ref),
            ("post_gain", post_gain_hbm, post_gain_ref),
            ("dec_gain", dec_gain_hbm, dec_gain_ref),
            ("wkv", wkv_hbm, wkv_ref),
            ("order", order_hbm, order_ref),
            ("queries", queries_hbm, queries_ref),
            ("head", head_hbm, head_ref.at[pl.ds(0, TILE)]),
        )
    ):
        loads[name] = pltpu.make_async_copy(source, target, local_sem.at[place])
        loads[name].start()

    def loaded(*names):
        for name in names:
            loads[name].wait()

    loaded("offset")
    offset = offset_ref[0]
    head_ref[pl.ds(TILE, 128 - TILE), :] = jnp.zeros((128 - TILE, WIDTH), BF16)

    cell = lax.broadcasted_iota(jnp.int32, (OWN, 1), 0)
    rest = jnp.where(cell >= TOKENS, cell - TOKENS, cell)
    line = over_twelve(rest)
    col = rest - 12 * line
    upper = col[:TOKENS] >= 12 - offset
    turned_col = col + jnp.where(cell >= TOKENS, 12, 0) + offset
    turned_col = 24 * line + jnp.where(turned_col >= 24, turned_col - 24, turned_col)
    cells = lax.broadcasted_iota(jnp.int32, (OWN, OWN), 1)
    turn = jnp.where(cells == turned_col, 1.0, 0.0).astype(BF16)
    loaded("latents")
    turned_ref[...] = dot_nn(turn, own_ref[...]).astype(BF16)

    pl.semaphore_wait(barrier, 2 + lev_count - 1)
    halo_copies = []
    for place, side in enumerate((east, west)):
        copy = pltpu.make_async_remote_copy(
            src_ref=turned_ref.at[pl.ds(TOKENS, TOKENS)],
            dst_ref=halo_ref.at[place],
            send_sem=halo_send_sem.at[place],
            recv_sem=halo_receive_sem.at[place],
            device_id=(side, lev),
            device_id_type=mesh_id,
        )
        copy.start()
        halo_copies.append(copy)

    lane24 = lax.broadcasted_iota(jnp.int32, (24, 128), 1)
    loaded("coords", "first", "first_offset", "second", "compact")
    second_high, second_low = split(second_ref[...])
    second_both = jnp.concatenate([second_high, second_low], axis=0)
    flat_part = (
        coords_ref[:, 0:1] * first_ref[1:2, :]
        + coords_ref[:, 1:2] * first_ref[2:3, :]
        + first_offset_ref[...]
    )
    for a in range(3):
        depth_coord = float(coordinate(np.float64((1 - a) * 8.0)))
        hidden = jnp.maximum(flat_part + depth_coord * first_ref[0:1, :], 0.0)
        hidden_high, hidden_low = split(hidden)
        both = dot_nt(second_both, hidden_high)
        logits = both[:HEADS] + both[HEADS:] + dot_nt(second_high, hidden_low)
        table = (16.0 * LOG2E) / (1.0 + jnp.exp(-logits))
        for x in range(12):
            rolled = table if x == 11 else pltpu.roll(table, 256 - (11 - x), 1)
            high, low = split(rolled)
            shifted_ref[pl.ds(x * HEADS, HEADS), :] = high
            shifted_ref[pl.ds((12 + x) * HEADS, HEADS), :] = low
        spread_out = dot_nn(shifted_ref[...], compact_ref[...])
        spread_out = spread_out[:192] + spread_out[192:]
        lattice_ref[a, pl.ds(0, 192), :] = spread_out[:, :128]
        lattice_ref[a, pl.ds(192, 192), :] = spread_out[:, 128:]

    for h in range(HEADS):
        lattice = [lattice_ref[a, pl.ds(h, 24, stride=HEADS), :] for a in range(3)]
        for dz in range(2):
            for m in range(3):
                start = (4 - 2 * m) * 12
                rows = pl.ds(72 * dz + 24 * m, 24)
                near = lattice[1 - dz]
                if start:
                    near = pltpu.roll(near, 128 - start, 1)
                far = pltpu.roll(lattice[2 - dz], 72 - start, 1)
                bias_ref[h, rows, :128] = jnp.where(lane24 < 72, near, far)
                bias_ref[h, rows, 128:] = far[:, :16]

    loaded("wqkv")
    turned = turned_ref[...]
    scale = LOG2E / math.sqrt(HEAD_DIM)
    packed_ref[:, :WIDTH] = (dot_nn(turned, wqkv_ref[:, :WIDTH]) * scale).astype(BF16)
    packed_ref[:, WIDTH:] = dot_nn(turned, wqkv_ref[:, WIDTH:]).astype(BF16)

    def soft(scores):
        raised = jnp.exp2(scores - jnp.max(scores, axis=-1, keepdims=True))
        total = jnp.sum(raised, axis=-1, keepdims=True)
        return (raised * pl.reciprocal(total, approx=True)).astype(BF16)

    loaded("wproj", "post_gain", "dec_gain", "wkv", "order", "queries", "head")
    head_lane = lax.broadcasted_iota(jnp.int32, (HEADS, WIDTH), 1) // HEAD_DIM
    head_row = lax.broadcasted_iota(jnp.int32, (HEADS, WIDTH), 0)
    for i in range(8):
        query = queries_ref[pl.ds(order_ref[i], 1), :]
        level_query_ref[pl.ds(i * HEADS, HEADS), :] = jnp.where(
            head_lane == head_row, query, 0.0
        ).astype(BF16)
    expand_ref[...] = jnp.where(
        lax.broadcasted_iota(jnp.int32, (256, WIDTH), 0) % HEADS
        == lax.broadcasted_iota(jnp.int32, (256, WIDTH), 1) // HEAD_DIM,
        1.0,
        0.0,
    ).astype(BF16)
    lane48 = lax.broadcasted_iota(jnp.int32, (48, 128), 1)
    level_lane = lax.broadcasted_iota(jnp.int32, (72, 256), 1) % 128 // HEADS
    tile_copies = ([], [])

    def piece(parts):
        tile = parts[0][1]
        for start, part in parts[1:]:
            tile = jnp.where(lane48 >= start, part, tile)
        return tile

    def finish(half, groups):
        mine = pl.ds(TOKENS * half, TOKENS)
        projected = dot_nn(attended_ref[mine, :], wproj_ref[...])
        mixed = (turned_ref[mine, :].astype(F32) + post_gain_ref[...] * norm(projected)).astype(BF16)
        mixed_ref[mine, :] = mixed
        normed = (dec_gain_ref[...] * norm(mixed.astype(F32))).astype(BF16)
        keys = dot_nn(normed, wkv_ref[:, :WIDTH]).astype(BF16)
        values = dot_nn(normed, wkv_ref[:, WIDTH:]).astype(BF16).astype(F32)
        scores = dot_nt(keys, level_query_ref[...]) * (0.5 / math.sqrt(HEAD_DIM))
        upper_weight = 0.5 + 0.5 * jnp.tanh(scores[:72] - scores[72:])
        weight_high = upper_weight.astype(BF16).astype(F32)
        weight_both = jnp.concatenate([weight_high, upper_weight - weight_high], axis=1)
        value_lower = values[72:]
        value_step = values[:72] - value_lower
        for group in groups:
            targets = [lax.rem(lev + step, lev_count) for step in group]
            levels = [2 * target + j for target in targets for j in range(2)]
            picked = jnp.concatenate(
                [jnp.where(level_lane == level, weight_both, 0.0) for level in levels], axis=0
            ).astype(BF16)
            wide = dot_nn(picked, expand_ref[...])
            decoded = jnp.concatenate(
                [
                    value_lower + wide[72 * i : 72 * i + 72] * value_step
                    for i in range(len(levels))
                ],
                axis=0,
            ).astype(BF16)
            result = dot_nt(decoded, head_ref[...])
            for i, step in enumerate(group):
                result_ref[half, step] = result[TOKENS * i : TOKENS * i + TOKENS]
                slabs = []
                for x in range(3):
                    slab = result_ref[half, step, pl.ds(x, 48, stride=3), :]
                    slabs.append(pltpu.roll(slab, x * TILE % 128, 1) if x else slab)
                block = jnp.concatenate(
                    [
                        piece([(0, slabs[0]), (TILE, slabs[1])]),
                        piece([(0, slabs[1]), (2 * TILE - 128, slabs[2])]),
                    ],
                    axis=1,
                ).astype(BF16)
                if step == 0:
                    receive_ref[half, pl.ds(lev, 1)] = block[None]
                    continue
                send_ref[half, step - 1] = block
                copy = pltpu.make_async_remote_copy(
                    src_ref=send_ref.at[half, step - 1],
                    dst_ref=receive_ref.at[half, lev],
                    send_sem=tile_send_sem.at[half, step - 1],
                    recv_sem=tile_receive_sem.at[half, step - 1],
                    device_id=(lon, targets[i]),
                    device_id_type=mesh_id,
                )
                copy.start()
                tile_copies[half].append(copy)

    lane128 = lax.broadcasted_iota(jnp.int32, (TOKENS, 128), 1)
    inner = pl.ds(0, TOKENS)
    zero = jnp.zeros((), BF16)
    for quad in range(4):
        q_inner = packed_ref[inner, pl.ds(128 * quad, 128)]
        k_inner = packed_ref[inner, pl.ds(WIDTH + 128 * quad, 128)]
        v_inner = packed_ref[inner, pl.ds(2 * WIDTH + 128 * quad, 128)]
        out = jnp.zeros((TOKENS, 128), F32)
        for j in range(4):
            mine = lane128 // HEAD_DIM == j
            weights = soft(dot_nt(jnp.where(mine, q_inner, zero), k_inner) + bias_ref[4 * quad + j])
            out = jnp.where(mine, dot_nn(weights, v_inner), out)
        attended_ref[inner, pl.ds(128 * quad, 128)] = out.astype(BF16)

    finish(0, ((2, 3, 1, 0),))

    for copy in halo_copies:
        copy.wait()
    halo = jnp.where(upper, halo_ref[1].astype(F32), halo_ref[0].astype(F32)).astype(BF16)
    packed_halo_ref[...] = dot_nn(halo, wqkv_ref[:, WIDTH:]).astype(BF16)
    lane256 = lax.broadcasted_iota(jnp.int32, (TOKENS, 256), 1)
    edge = pl.ds(TOKENS, TOKENS)
    for quad in range(4):
        q_edge = packed_ref[edge, pl.ds(128 * quad, 128)].astype(F32)
        k_edge = packed_ref[edge, pl.ds(WIDTH + 128 * quad, 128)].astype(F32)
        v_edge = packed_ref[edge, pl.ds(2 * WIDTH + 128 * quad, 128)].astype(F32)
        k_halo = packed_halo_ref[:, pl.ds(128 * quad, 128)].astype(F32)
        v_halo = packed_halo_ref[:, pl.ds(WIDTH + 128 * quad, 128)].astype(F32)
        q_both = jnp.concatenate([jnp.where(upper, q_edge, 0.0), jnp.where(upper, 0.0, q_edge)], 1)
        k_both = jnp.concatenate(
            [jnp.where(upper, k_edge, k_halo), jnp.where(upper, k_halo, k_edge)], 1
        )
        v_both = jnp.concatenate(
            [jnp.where(upper, v_edge, v_halo), jnp.where(upper, v_halo, v_edge)], 1
        )
        q_both, k_both, v_both = q_both.astype(BF16), k_both.astype(BF16), v_both.astype(BF16)
        out_upper = jnp.zeros((TOKENS, 128), F32)
        out_lower = jnp.zeros((TOKENS, 128), F32)
        for j in range(4):
            mine = lane256 % 128 // HEAD_DIM == j
            weights = soft(dot_nt(jnp.where(mine, q_both, zero), k_both) + bias_ref[4 * quad + j])
            both = dot_nn(weights, v_both)
            mine = lane128 // HEAD_DIM == j
            out_upper = jnp.where(mine, both[:, :128], out_upper)
            out_lower = jnp.where(mine, both[:, 128:], out_lower)
        out = jnp.where(upper, out_upper, out_lower)
        attended_ref[edge, pl.ds(128 * quad, 128)] = out.astype(BF16)

    finish(1, ((2, 3), (1, 0)))

    own_line = over_twelve(lax.shift_right_logical(cell, 1))
    back_col = cell - 24 * own_line - offset
    back_col = jnp.where(back_col < 0, back_col + 24, back_col)
    back_col = 12 * own_line + jnp.where(back_col >= 12, back_col + (TOKENS - 12), back_col)
    turn_back = jnp.where(cells == back_col, 1.0, 0.0).astype(BF16)
    hidden_ref[...] = dot_nn(turn_back, mixed_ref[...]).astype(BF16)

    rows = 48 * lev_count
    slot_row = lax.broadcasted_iota(jnp.int32, (48, 1), 0)
    slot = jnp.where(slot_row >= 24, 1, 0)
    lat = slot_row - 24 * slot
    source = over_twelve(2 * lat)
    base = 48 * source + 24 * slot + 4 * (lat - 6 * source)
    place = lax.broadcasted_iota(jnp.int32, (48, rows), 1) - base
    gather = jnp.concatenate([jnp.where(place == q, 1.0, 0.0) for q in range(4)], 0).astype(BF16)
    parts = [[] for _ in range(ROW // 128)]
    for half in range(2):
        for copy in tile_copies[half]:
            copy.wait()
        sorted_rows = dot_nn(gather, receive_ref[half].reshape(rows, 256))
        for q in range(4):
            for c in range(2):
                part = sorted_rows[48 * q : 48 * q + 48, 128 * c : 128 * c + 128]
                first = 960 * half + 240 * q + 128 * c
                if first % 128:
                    part = pltpu.roll(part, first % 128, 1)
                last = first + (127 if c == 0 else 111)
                for k in range(first // 128, last // 128 + 1):
                    parts[k].append((first - 128 * k, part))
    shift = TILE * offset
    count = ROW // 128
    tiles = [piece(part).astype(BF16) for part in parts]
    pairs = jnp.concatenate(
        [jnp.concatenate([tiles[k - 1], tiles[k]], axis=1) for k in range(count)], axis=0
    )
    slide = lax.broadcasted_iota(jnp.int32, (256, 128), 0) - lax.broadcasted_iota(
        jnp.int32, (256, 128), 1
    )
    slide = jnp.where(slide == 128 - (shift & 127), 1.0, 0.0).astype(BF16)
    turned_lanes = dot_nn(pairs, slide)
    tiles = [turned_lanes[48 * k : 48 * k + 48] for k in range(count)]
    whole = jnp.zeros((48, 128), jnp.int32) + lax.shift_right_logical(shift, 7)
    for bit in (1, 2, 4):
        chosen = whole & bit != 0
        tiles = [jnp.where(chosen, tiles[k - bit], tiles[k]) for k in range(count)]
    for k in range(count):
        tiles_ref[:, pl.ds(128 * k, 128)] = tiles[k].astype(BF16)


def body(
    latents,
    shift_offset,
    qkv_weight,
    proj_weight,
    post_gain,
    bias_first_weight,
    bias_first_offset,
    bias_second_weight,
    dec_gain,
    kv_weight,
    head_weight,
    level_queries,
    level_order,
):
    lon_count = lax.axis_size("lon")
    lev_count = lax.axis_size("lev")
    coords, compact = constants()
    vmem = pl.BlockSpec(memory_space=pltpu.VMEM)
    hbm = pl.BlockSpec(memory_space=pltpu.HBM)
    dma = pltpu.SemaphoreType.DMA
    hidden, tiles = pl.pallas_call(
        functools.partial(kernel, lon_count, lev_count),
        out_shape=(
            jax.ShapeDtypeStruct((OWN, WIDTH), BF16),
            jax.ShapeDtypeStruct((48, ROW), BF16),
        ),
        in_specs=[hbm] * 15,
        out_specs=(vmem, vmem),
        scratch_shapes=[
            pltpu.SMEM((1,), jnp.int32),
            pltpu.SMEM((8,), jnp.int32),
            pltpu.VMEM((OWN, WIDTH), BF16),
            pltpu.VMEM((WIDTH, 3 * WIDTH), BF16),
            pltpu.VMEM((WIDTH, WIDTH), BF16),
            pltpu.VMEM((WIDTH, 2 * WIDTH), BF16),
            pltpu.VMEM((1, WIDTH), F32),
            pltpu.VMEM((3, WIDTH), F32),
            pltpu.VMEM((1, WIDTH), F32),
            pltpu.VMEM((HEADS, WIDTH), F32),
            pltpu.VMEM((1, WIDTH), F32),
            pltpu.VMEM((128, WIDTH), BF16),
            pltpu.VMEM((8, WIDTH), F32),
            pltpu.VMEM((256, 2), F32),
            pltpu.VMEM((256, 256), BF16),
            pltpu.VMEM((OWN, WIDTH), BF16),
            pltpu.VMEM((2, TOKENS, WIDTH), BF16),
            pltpu.VMEM((384, 256), BF16),
            pltpu.VMEM((3, 384, 128), F32),
            pltpu.VMEM((HEADS, TOKENS, TOKENS), F32),
            pltpu.VMEM((OWN, 3 * WIDTH), BF16),
            pltpu.VMEM((TOKENS, 2 * WIDTH), BF16),
            pltpu.VMEM((OWN, WIDTH), BF16),
            pltpu.VMEM((OWN, WIDTH), BF16),
            pltpu.VMEM((128, WIDTH), BF16),
            pltpu.VMEM((256, WIDTH), BF16),
            pltpu.VMEM((2, lev_count, TOKENS, 128), F32),
            pltpu.VMEM((2, lev_count - 1, 48, 256), BF16),
            pltpu.VMEM((2, lev_count, 48, 256), BF16),
            dma((15,)),
            dma((2,)),
            dma((2,)),
            dma((2, lev_count - 1)),
            dma((2, lev_count - 1)),
        ],
        compiler_params=pltpu.CompilerParams(
            collective_id=0, has_side_effects=True, vmem_limit_bytes=40 * 1024 * 1024
        ),
    )(
        shift_offset,
        *(
            pltpu.with_memory_space_constraint(value, pltpu.HBM)
            for value in (
                level_order,
                latents.reshape(OWN, WIDTH),
                qkv_weight,
                proj_weight,
                kv_weight,
                post_gain.reshape(1, WIDTH),
                bias_first_weight,
                bias_first_offset.reshape(1, WIDTH),
                bias_second_weight.T,
                dec_gain.reshape(1, WIDTH),
                head_weight.T,
                level_queries,
                jnp.asarray(coords),
                jnp.asarray(compact),
            )
        )
    )
    return hidden.reshape(latents.shape), tiles.reshape(2, 24, ROW)


def solution(mesh):
    return jax.shard_map(
        body,
        mesh=mesh,
        in_specs=(P(None, "lev", "lon", None),) + (P(),) * 12,
        out_specs=(P(None, "lev", "lon", None), P("lev", None, "lon")),
        check_vma=False,
    )
```

```python
import functools
import math

import jax
import jax.numpy as jnp
import numpy as np
from jax import lax
from jax.experimental import pallas as pl
from jax.experimental.pallas import tpu as pltpu
from jax.sharding import PartitionSpec as P

EPSILON = 1e-05
WIDTH = 512
HEADS = 16
HEAD_DIM = WIDTH // HEADS
TOKENS = 144
OWN = 288
TILE = 80
ROW = 24 * TILE
LOG2E = math.log2(math.e)
BF16 = jnp.bfloat16
F32 = jnp.float32


def dot_nn(a, b):
    return lax.dot_general(a, b, (((1,), (0,)), ((), ())), preferred_element_type=F32)


def dot_nt(a, b):
    return lax.dot_general(a, b, (((1,), (1,)), ((), ())), preferred_element_type=F32)


def split(value):
    high = value.astype(BF16)
    return high, (value - high.astype(F32)).astype(BF16)


def coordinate(steps):
    return np.sign(steps) * np.log2(np.abs(steps) + 1.0) / 3.0


def constants():
    place = np.arange(256)
    row, col = place // 23, place % 23
    inside = place < 253
    coords = np.zeros((256, 2), np.float32)
    coords[:, 0] = np.where(inside, coordinate((5 - row) * 8.0 / 5.0), 0.0)
    coords[:, 1] = np.where(inside, coordinate((11 - col) * 8.0 / 11.0), 0.0)
    compact = np.zeros((256, 256), np.float32)
    for part in range(2):
        for k in range(10):
            for x in range(12):
                compact[(k + 1 - part) * 23 + x, part * 128 + 12 * k + x] = 1.0
    return coords, compact.astype(BF16)


def over_twelve(value):
    return lax.shift_right_logical(value * 43691, 19)


def norm(values):
    centre = values - jnp.mean(values, axis=-1, keepdims=True)
    spread = jnp.mean(centre * centre, axis=-1, keepdims=True)
    return centre * lax.rsqrt(spread + EPSILON)


def kernel(
    lon_count,
    lev_count,
    offset_hbm,
    order_hbm,
    latents_hbm,
    wqkv_hbm,
    wproj_hbm,
    wkv_hbm,
    post_gain_hbm,
    first_hbm,
    first_offset_hbm,
    second_hbm,
    dec_gain_hbm,
    head_hbm,
    queries_hbm,
    coords_hbm,
    compact_hbm,
    hidden_ref,
    tiles_ref,
    offset_ref,
    order_ref,
    own_ref,
    wqkv_ref,
    wproj_ref,
    wkv_ref,
    post_gain_ref,
    first_ref,
    first_offset_ref,
    second_ref,
    dec_gain_ref,
    head_ref,
    queries_ref,
    coords_ref,
    compact_ref,
    turned_ref,
    halo_ref,
    shifted_ref,
    lattice_ref,
    bias_ref,
    packed_ref,
    packed_halo_ref,
    attended_ref,
    share_ref,
    mixed_ref,
    level_query_ref,
    expand_ref,
    result_ref,
    send_ref,
    receive_ref,
    local_sem,
    halo_send_sem,
    halo_receive_sem,
    tile_send_sem,
    tile_receive_sem,
):
    lon = lax.axis_index("lon")
    lev = lax.axis_index("lev")
    west = lax.rem(lon + lon_count - 1, lon_count)
    east = lax.rem(lon + 1, lon_count)
    mesh_id = pl.DeviceIdType.MESH

    barrier = pltpu.get_barrier_semaphore()
    for side in (west, east):
        pl.semaphore_signal(barrier, inc=1, device_id=(side, lev), device_id_type=mesh_id)
    for step in range(1, lev_count):
        pl.semaphore_signal(
            barrier,
            inc=1,
            device_id=(lon, lax.rem(lev + step, lev_count)),
            device_id_type=mesh_id,
        )

    loads = {}
    for place, (name, source, target) in enumerate(
        (
            ("offset", offset_hbm, offset_ref),
            ("latents", latents_hbm, own_ref),
            ("coords", coords_hbm, coords_ref),
            ("first", first_hbm, first_ref),
            ("first_offset", first_offset_hbm, first_offset_ref),
            ("second", second_hbm, second_ref),
            ("compact", compact_hbm, compact_ref),
            ("wqkv", wqkv_hbm, wqkv_ref),
            ("wproj", wproj_hbm, wproj_ref),
            ("post_gain", post_gain_hbm, post_gain_ref),
            ("dec_gain", dec_gain_hbm, dec_gain_ref),
            ("wkv", wkv_hbm, wkv_ref),
            ("order", order_hbm, order_ref),
            ("queries", queries_hbm, queries_ref),
            ("head", head_hbm, head_ref.at[pl.ds(0, TILE)]),
        )
    ):
        loads[name] = pltpu.make_async_copy(source, target, local_sem.at[place])
        loads[name].start()

    def loaded(*names):
        for name in names:
            loads[name].wait()

    loaded("offset")
    offset = offset_ref[0]
    head_ref[pl.ds(TILE, 128 - TILE), :] = jnp.zeros((128 - TILE, WIDTH), BF16)

    cell = lax.broadcasted_iota(jnp.int32, (OWN, 1), 0)
    rest = jnp.where(cell >= TOKENS, cell - TOKENS, cell)
    line = over_twelve(rest)
    col = rest - 12 * line
    upper = col[:TOKENS] >= 12 - offset
    turned_col = col + jnp.where(cell >= TOKENS, 12, 0) + offset
    turned_col = 24 * line + jnp.where(turned_col >= 24, turned_col - 24, turned_col)
    cells = lax.broadcasted_iota(jnp.int32, (OWN, OWN), 1)
    turn = jnp.where(cells == turned_col, 1.0, 0.0).astype(BF16)
    loaded("latents")
    turned_ref[...] = dot_nn(turn, own_ref[...]).astype(BF16)

    pl.semaphore_wait(barrier, 2 + lev_count - 1)
    halo_copies = []
    for place, side in enumerate((east, west)):
        copy = pltpu.make_async_remote_copy(
            src_ref=turned_ref.at[pl.ds(TOKENS, TOKENS)],
            dst_ref=halo_ref.at[place],
            send_sem=halo_send_sem.at[place],
            recv_sem=halo_receive_sem.at[place],
            device_id=(side, lev),
            device_id_type=mesh_id,
        )
        copy.start()
        halo_copies.append(copy)

    lane24 = lax.broadcasted_iota(jnp.int32, (24, 128), 1)
    loaded("coords", "first", "first_offset", "second", "compact")
    second_high, second_low = split(second_ref[...])
    second_both = jnp.concatenate([second_high, second_low], axis=0)
    flat_part = (
        coords_ref[:, 0:1] * first_ref[1:2, :]
        + coords_ref[:, 1:2] * first_ref[2:3, :]
        + first_offset_ref[...]
    )
    for a in range(3):
        depth_coord = float(coordinate(np.float64((1 - a) * 8.0)))
        hidden = jnp.maximum(flat_part + depth_coord * first_ref[0:1, :], 0.0)
        hidden_high, hidden_low = split(hidden)
        both = dot_nt(second_both, hidden_high)
        logits = both[:HEADS] + both[HEADS:] + dot_nt(second_high, hidden_low)
        table = (16.0 * LOG2E) / (1.0 + jnp.exp(-logits))
        for x in range(12):
            rolled = table if x == 11 else pltpu.roll(table, 256 - (11 - x), 1)
            high, low = split(rolled)
            shifted_ref[pl.ds(x * HEADS, HEADS), :] = high
            shifted_ref[pl.ds((12 + x) * HEADS, HEADS), :] = low
        spread_out = dot_nn(shifted_ref[...], compact_ref[...])
        spread_out = spread_out[:192] + spread_out[192:]
        lattice_ref[a, pl.ds(0, 192), :] = spread_out[:, :128]
        lattice_ref[a, pl.ds(192, 192), :] = spread_out[:, 128:]

    for h in range(HEADS):
        lattice = [lattice_ref[a, pl.ds(h, 24, stride=HEADS), :] for a in range(3)]
        for dz in range(2):
            for m in range(3):
                start = (4 - 2 * m) * 12
                rows = pl.ds(72 * dz + 24 * m, 24)
                near = lattice[1 - dz]
                if start:
                    near = pltpu.roll(near, 128 - start, 1)
                far = pltpu.roll(lattice[2 - dz], 72 - start, 1)
                bias_ref[h, rows, :128] = jnp.where(lane24 < 72, near, far)
                bias_ref[h, rows, 128:] = far[:, :16]

    loaded("wqkv")
    turned = turned_ref[...]
    scale = LOG2E / math.sqrt(HEAD_DIM)
    packed_ref[:, :WIDTH] = (dot_nn(turned, wqkv_ref[:, :WIDTH]) * scale).astype(BF16)
    packed_ref[:, WIDTH:] = dot_nn(turned, wqkv_ref[:, WIDTH:]).astype(BF16)

    def soft(scores):
        raised = jnp.exp2(scores - jnp.max(scores, axis=-1, keepdims=True))
        total = jnp.sum(raised, axis=-1, keepdims=True)
        return (raised * pl.reciprocal(total, approx=True)).astype(BF16)

    loaded("wproj", "post_gain", "dec_gain", "wkv", "order", "queries", "head")
    head_lane = lax.broadcasted_iota(jnp.int32, (HEADS, WIDTH), 1) // HEAD_DIM
    head_row = lax.broadcasted_iota(jnp.int32, (HEADS, WIDTH), 0)
    for i in range(8):
        query = queries_ref[pl.ds(order_ref[i], 1), :]
        level_query_ref[pl.ds(i * HEADS, HEADS), :] = jnp.where(
            head_lane == head_row, query, 0.0
        ).astype(BF16)
    expand_ref[...] = jnp.where(
        lax.broadcasted_iota(jnp.int32, (256, WIDTH), 0) % HEADS
        == lax.broadcasted_iota(jnp.int32, (256, WIDTH), 1) // HEAD_DIM,
        1.0,
        0.0,
    ).astype(BF16)
    lane48 = lax.broadcasted_iota(jnp.int32, (48, 128), 1)
    level_lane = lax.broadcasted_iota(jnp.int32, (72, 256), 1) % 128 // HEADS
    tile_copies = ([], [])

    def piece(parts):
        tile = parts[0][1]
        for start, part in parts[1:]:
            tile = jnp.where(lane48 >= start, part, tile)
        return tile

    def finish(half, groups):
        mine = pl.ds(TOKENS * half, TOKENS)
        projected = dot_nn(attended_ref[mine, :], wproj_ref[...])
        mixed = (turned_ref[mine, :].astype(F32) + post_gain_ref[...] * norm(projected)).astype(BF16)
        mixed_ref[mine, :] = mixed
        normed = (dec_gain_ref[...] * norm(mixed.astype(F32))).astype(BF16)
        keys = dot_nn(normed, wkv_ref[:, :WIDTH]).astype(BF16)
        values = dot_nn(normed, wkv_ref[:, WIDTH:]).astype(BF16).astype(F32)
        scores = dot_nt(keys, level_query_ref[...]) * (0.5 / math.sqrt(HEAD_DIM))
        upper_weight = 0.5 + 0.5 * jnp.tanh(scores[:72] - scores[72:])
        weight_high = upper_weight.astype(BF16).astype(F32)
        weight_both = jnp.concatenate([weight_high, upper_weight - weight_high], axis=1)
        value_lower = values[72:]
        value_step = values[:72] - value_lower
        for group in groups:
            targets = [lax.rem(lev + step, lev_count) for step in group]
            levels = [2 * target + j for target in targets for j in range(2)]
            picked = jnp.concatenate(
                [jnp.where(level_lane == level, weight_both, 0.0) for level in levels], axis=0
            ).astype(BF16)
            wide = dot_nn(picked, expand_ref[...])
            decoded = jnp.concatenate(
                [
                    value_lower + wide[72 * i : 72 * i + 72] * value_step
                    for i in range(len(levels))
                ],
                axis=0,
            ).astype(BF16)
            result = dot_nt(decoded, head_ref[...])
            for i, step in enumerate(group):
                result_ref[half, step] = result[TOKENS * i : TOKENS * i + TOKENS]
                slabs = []
                for x in range(3):
                    slab = result_ref[half, step, pl.ds(x, 48, stride=3), :]
                    slabs.append(pltpu.roll(slab, x * TILE % 128, 1) if x else slab)
                block = jnp.concatenate(
                    [
                        piece([(0, slabs[0]), (TILE, slabs[1])]),
                        piece([(0, slabs[1]), (2 * TILE - 128, slabs[2])]),
                    ],
                    axis=1,
                ).astype(BF16)
                if step == 0:
                    receive_ref[half, pl.ds(lev, 1)] = block[None]
                    continue
                send_ref[half, step - 1] = block
                copy = pltpu.make_async_remote_copy(
                    src_ref=send_ref.at[half, step - 1],
                    dst_ref=receive_ref.at[half, lev],
                    send_sem=tile_send_sem.at[half, step - 1],
                    recv_sem=tile_receive_sem.at[half, step - 1],
                    device_id=(lon, targets[i]),
                    device_id_type=mesh_id,
                )
                copy.start()
                tile_copies[half].append(copy)

    lane128 = lax.broadcasted_iota(jnp.int32, (TOKENS, 128), 1)
    inner = pl.ds(0, TOKENS)
    zero = jnp.zeros((), BF16)
    for quad in range(4):
        q_inner = packed_ref[inner, pl.ds(128 * quad, 128)]
        k_inner = packed_ref[inner, pl.ds(WIDTH + 128 * quad, 128)]
        v_inner = packed_ref[inner, pl.ds(2 * WIDTH + 128 * quad, 128)]
        q_heads = jnp.concatenate(
            [jnp.where(lane128 // HEAD_DIM == j, q_inner, zero) for j in range(4)], axis=0
        )
        bias = bias_ref[pl.ds(4 * quad, 4)].reshape(4 * TOKENS, TOKENS)
        heads = dot_nn(soft(dot_nt(q_heads, k_inner) + bias), v_inner)
        out = heads[:TOKENS]
        for j in range(1, 4):
            part = heads[TOKENS * j : TOKENS * j + TOKENS]
            out = jnp.where(lane128 // HEAD_DIM == j, part, out)
        attended_ref[inner, pl.ds(128 * quad, 128)] = out.astype(BF16)

    lane = lax.broadcasted_iota(jnp.int32, (1, TOKENS), 1)
    upper_key = lane - 12 * over_twelve(lane) >= 12 - offset
    side = jnp.where(upper, 1, 0) + jnp.zeros((TOKENS, TOKENS), jnp.int32)
    same = side == jnp.where(upper_key, 1, 0)
    edge = pl.ds(TOKENS, TOKENS)

    def by_head(rows):
        out = rows(0)
        for j in range(1, 4):
            out = jnp.where(lane128 // HEAD_DIM == j, rows(j), out)
        return out

    def share(quad, keys, values, met):
        query = packed_ref[edge, pl.ds(128 * quad, 128)]
        q_heads = jnp.concatenate(
            [jnp.where(lane128 // HEAD_DIM == j, query, zero) for j in range(4)], axis=0
        )
        bias = jnp.where(met[None], bias_ref[pl.ds(4 * quad, 4)], -1e30)
        scores = dot_nt(q_heads, keys) + bias.reshape(4 * TOKENS, TOKENS)
        peak = jnp.max(scores, axis=-1, keepdims=True)
        raised = jnp.exp2(scores - peak)
        total = jnp.sum(raised, axis=-1, keepdims=True)
        heads = dot_nn(raised.astype(BF16), values)
        return [
            by_head(lambda j: value[TOKENS * j : TOKENS * j + TOKENS])
            for value in (peak, total, heads)
        ]

    for quad in range(4):
        found = share(
            quad,
            packed_ref[edge, pl.ds(WIDTH + 128 * quad, 128)],
            packed_ref[edge, pl.ds(2 * WIDTH + 128 * quad, 128)],
            same,
        )
        for i in range(3):
            share_ref[i, :, pl.ds(128 * quad, 128)] = found[i]

    finish(0, ((2, 3, 1, 0),))

    for copy in halo_copies:
        copy.wait()
    halo = jnp.where(upper, halo_ref[1].astype(F32), halo_ref[0].astype(F32)).astype(BF16)
    packed_halo_ref[...] = dot_nn(halo, wqkv_ref[:, WIDTH:]).astype(BF16)
    for quad in range(4):
        lanes = pl.ds(128 * quad, 128)
        far_peak, far_total, far_out = share(
            quad,
            packed_halo_ref[:, lanes],
            packed_halo_ref[:, pl.ds(WIDTH + 128 * quad, 128)],
            jnp.logical_not(same),
        )
        near_peak = share_ref[0, :, lanes]
        peak = jnp.maximum(near_peak, far_peak)
        near_scale = jnp.exp2(near_peak - peak)
        far_scale = jnp.exp2(far_peak - peak)
        total = share_ref[1, :, lanes] * near_scale + far_total * far_scale
        out = (share_ref[2, :, lanes] * near_scale + far_out * far_scale) / total
        attended_ref[edge, lanes] = out.astype(BF16)

    finish(1, ((2, 3), (1, 0)))

    own_line = over_twelve(lax.shift_right_logical(cell, 1))
    back_col = cell - 24 * own_line - offset
    back_col = jnp.where(back_col < 0, back_col + 24, back_col)
    back_col = 12 * own_line + jnp.where(back_col >= 12, back_col + (TOKENS - 12), back_col)
    turn_back = jnp.where(cells == back_col, 1.0, 0.0).astype(BF16)
    hidden_ref[...] = dot_nn(turn_back, mixed_ref[...]).astype(BF16)

    rows = 48 * lev_count
    slot_row = lax.broadcasted_iota(jnp.int32, (48, 1), 0)
    slot = jnp.where(slot_row >= 24, 1, 0)
    lat = slot_row - 24 * slot
    source = over_twelve(2 * lat)
    base = 48 * source + 24 * slot + 4 * (lat - 6 * source)
    place = lax.broadcasted_iota(jnp.int32, (48, rows), 1) - base
    gather = jnp.concatenate([jnp.where(place == q, 1.0, 0.0) for q in range(4)], 0).astype(BF16)
    parts = [[] for _ in range(ROW // 128)]
    for half in range(2):
        for copy in tile_copies[half]:
            copy.wait()
        sorted_rows = dot_nn(gather, receive_ref[half].reshape(rows, 256))
        for q in range(4):
            for c in range(2):
                part = sorted_rows[48 * q : 48 * q + 48, 128 * c : 128 * c + 128]
                first = 960 * half + 240 * q + 128 * c
                if first % 128:
                    part = pltpu.roll(part, first % 128, 1)
                last = first + (127 if c == 0 else 111)
                for k in range(first // 128, last // 128 + 1):
                    parts[k].append((first - 128 * k, part))
    shift = TILE * offset
    count = ROW // 128
    tiles = [piece(part).astype(BF16) for part in parts]
    pairs = jnp.concatenate(
        [jnp.concatenate([tiles[k - 1], tiles[k]], axis=1) for k in range(count)], axis=0
    )
    slide = lax.broadcasted_iota(jnp.int32, (256, 128), 0) - lax.broadcasted_iota(
        jnp.int32, (256, 128), 1
    )
    slide = jnp.where(slide == 128 - (shift & 127), 1.0, 0.0).astype(BF16)
    turned_lanes = dot_nn(pairs, slide)
    tiles = [turned_lanes[48 * k : 48 * k + 48] for k in range(count)]
    whole = jnp.zeros((48, 128), jnp.int32) + lax.shift_right_logical(shift, 7)
    for bit in (1, 2, 4):
        chosen = whole & bit != 0
        tiles = [jnp.where(chosen, tiles[k - bit], tiles[k]) for k in range(count)]
    for k in range(count):
        tiles_ref[:, pl.ds(128 * k, 128)] = tiles[k].astype(BF16)


def body(
    latents,
    shift_offset,
    qkv_weight,
    proj_weight,
    post_gain,
    bias_first_weight,
    bias_first_offset,
    bias_second_weight,
    dec_gain,
    kv_weight,
    head_weight,
    level_queries,
    level_order,
):
    lon_count = lax.axis_size("lon")
    lev_count = lax.axis_size("lev")
    coords, compact = constants()
    vmem = pl.BlockSpec(memory_space=pltpu.VMEM)
    hbm = pl.BlockSpec(memory_space=pltpu.HBM)
    dma = pltpu.SemaphoreType.DMA
    hidden, tiles = pl.pallas_call(
        functools.partial(kernel, lon_count, lev_count),
        out_shape=(
            jax.ShapeDtypeStruct((OWN, WIDTH), BF16),
            jax.ShapeDtypeStruct((48, ROW), BF16),
        ),
        in_specs=[hbm] * 15,
        out_specs=(vmem, vmem),
        scratch_shapes=[
            pltpu.SMEM((1,), jnp.int32),
            pltpu.SMEM((8,), jnp.int32),
            pltpu.VMEM((OWN, WIDTH), BF16),
            pltpu.VMEM((WIDTH, 3 * WIDTH), BF16),
            pltpu.VMEM((WIDTH, WIDTH), BF16),
            pltpu.VMEM((WIDTH, 2 * WIDTH), BF16),
            pltpu.VMEM((1, WIDTH), F32),
            pltpu.VMEM((3, WIDTH), F32),
            pltpu.VMEM((1, WIDTH), F32),
            pltpu.VMEM((HEADS, WIDTH), F32),
            pltpu.VMEM((1, WIDTH), F32),
            pltpu.VMEM((128, WIDTH), BF16),
            pltpu.VMEM((8, WIDTH), F32),
            pltpu.VMEM((256, 2), F32),
            pltpu.VMEM((256, 256), BF16),
            pltpu.VMEM((OWN, WIDTH), BF16),
            pltpu.VMEM((2, TOKENS, WIDTH), BF16),
            pltpu.VMEM((384, 256), BF16),
            pltpu.VMEM((3, 384, 128), F32),
            pltpu.VMEM((HEADS, TOKENS, TOKENS), F32),
            pltpu.VMEM((OWN, 3 * WIDTH), BF16),
            pltpu.VMEM((TOKENS, 2 * WIDTH), BF16),
            pltpu.VMEM((OWN, WIDTH), BF16),
            pltpu.VMEM((3, TOKENS, WIDTH), F32),
            pltpu.VMEM((OWN, WIDTH), BF16),
            pltpu.VMEM((128, WIDTH), BF16),
            pltpu.VMEM((256, WIDTH), BF16),
            pltpu.VMEM((2, lev_count, TOKENS, 128), F32),
            pltpu.VMEM((2, lev_count - 1, 48, 256), BF16),
            pltpu.VMEM((2, lev_count, 48, 256), BF16),
            dma((15,)),
            dma((2,)),
            dma((2,)),
            dma((2, lev_count - 1)),
            dma((2, lev_count - 1)),
        ],
        compiler_params=pltpu.CompilerParams(
            collective_id=0, has_side_effects=True, vmem_limit_bytes=40 * 1024 * 1024
        ),
    )(
        shift_offset,
        *(
            pltpu.with_memory_space_constraint(value, pltpu.HBM)
            for value in (
                level_order,
                latents.reshape(OWN, WIDTH),
                qkv_weight,
                proj_weight,
                kv_weight,
                post_gain.reshape(1, WIDTH),
                bias_first_weight,
                bias_first_offset.reshape(1, WIDTH),
                bias_second_weight.T,
                dec_gain.reshape(1, WIDTH),
                head_weight.T,
                level_queries,
                jnp.asarray(coords),
                jnp.asarray(compact),
            )
        )
    )
    return hidden.reshape(latents.shape), tiles.reshape(2, 24, ROW)


def solution(mesh):
    return jax.shard_map(
        body,
        mesh=mesh,
        in_specs=(P(None, "lev", "lon", None),) + (P(),) * 12,
        out_specs=(P(None, "lev", "lon", None), P("lev", None, "lon")),
        check_vma=False,
    )
```

```python
import functools
import math

import jax
import jax.numpy as jnp
import numpy as np
from jax import lax
from jax.experimental import pallas as pl
from jax.experimental.pallas import tpu as pltpu
from jax.sharding import PartitionSpec as P

EPSILON = 1e-05
WIDTH = 512
HEADS = 16
HEAD_DIM = WIDTH // HEADS
TOKENS = 144
OWN = 288
TILE = 80
ROW = 24 * TILE
LOG2E = math.log2(math.e)
BF16 = jnp.bfloat16
F32 = jnp.float32


def dot_nn(a, b):
    return lax.dot_general(a, b, (((1,), (0,)), ((), ())), preferred_element_type=F32)


def dot_nt(a, b):
    return lax.dot_general(a, b, (((1,), (1,)), ((), ())), preferred_element_type=F32)


def split(value):
    high = value.astype(BF16)
    return high, (value - high.astype(F32)).astype(BF16)


def coordinate(steps):
    return np.sign(steps) * np.log2(np.abs(steps) + 1.0) / 3.0


def constants():
    place = np.arange(256)
    row, col = place // 23, place % 23
    inside = place < 253
    coords = np.zeros((256, 2), np.float32)
    coords[:, 0] = np.where(inside, coordinate((5 - row) * 8.0 / 5.0), 0.0)
    coords[:, 1] = np.where(inside, coordinate((11 - col) * 8.0 / 11.0), 0.0)
    compact = np.zeros((256, 256), np.float32)
    for part in range(2):
        for k in range(10):
            for x in range(12):
                compact[(k + 1 - part) * 23 + x, part * 128 + 12 * k + x] = 1.0
    return coords, compact.astype(BF16)


def over_twelve(value):
    return lax.shift_right_logical(value * 43691, 19)


def norm(values):
    centre = values - jnp.mean(values, axis=-1, keepdims=True)
    spread = jnp.mean(centre * centre, axis=-1, keepdims=True)
    return centre * lax.rsqrt(spread + EPSILON)


def kernel(
    lon_count,
    lev_count,
    offset_hbm,
    order_hbm,
    latents_hbm,
    wqkv_hbm,
    wproj_hbm,
    wkv_hbm,
    post_gain_hbm,
    first_hbm,
    first_offset_hbm,
    second_hbm,
    dec_gain_hbm,
    head_hbm,
    queries_hbm,
    coords_hbm,
    compact_hbm,
    hidden_ref,
    tiles_ref,
    offset_ref,
    order_ref,
    own_ref,
    wqkv_ref,
    wproj_ref,
    wkv_ref,
    post_gain_ref,
    first_ref,
    first_offset_ref,
    second_ref,
    dec_gain_ref,
    head_ref,
    queries_ref,
    coords_ref,
    compact_ref,
    turned_ref,
    halo_ref,
    shifted_ref,
    lattice_ref,
    bias_ref,
    packed_ref,
    packed_halo_ref,
    attended_ref,
    share_ref,
    mixed_ref,
    level_query_ref,
    expand_ref,
    result_ref,
    send_ref,
    receive_ref,
    local_sem,
    halo_send_sem,
    halo_receive_sem,
    tile_send_sem,
    tile_receive_sem,
):
    lon = lax.axis_index("lon")
    lev = lax.axis_index("lev")
    west = lax.rem(lon + lon_count - 1, lon_count)
    east = lax.rem(lon + 1, lon_count)
    mesh_id = pl.DeviceIdType.MESH

    barrier = pltpu.get_barrier_semaphore()
    for side in (west, east):
        pl.semaphore_signal(barrier, inc=1, device_id=(side, lev), device_id_type=mesh_id)
    for step in range(1, lev_count):
        pl.semaphore_signal(
            barrier,
            inc=1,
            device_id=(lon, lax.rem(lev + step, lev_count)),
            device_id_type=mesh_id,
        )

    loads = {}
    for place, (name, source, target) in enumerate(
        (
            ("offset", offset_hbm, offset_ref),
            ("latents", latents_hbm, own_ref),
            ("coords", coords_hbm, coords_ref),
            ("first", first_hbm, first_ref),
            ("first_offset", first_offset_hbm, first_offset_ref),
            ("second", second_hbm, second_ref),
            ("compact", compact_hbm, compact_ref),
            ("wqkv", wqkv_hbm, wqkv_ref),
            ("wproj", wproj_hbm, wproj_ref),
            ("post_gain", post_gain_hbm, post_gain_ref),
            ("dec_gain", dec_gain_hbm, dec_gain_ref),
            ("wkv", wkv_hbm, wkv_ref),
            ("order", order_hbm, order_ref),
            ("queries", queries_hbm, queries_ref),
            ("head", head_hbm, head_ref.at[pl.ds(0, TILE)]),
        )
    ):
        loads[name] = pltpu.make_async_copy(source, target, local_sem.at[place])
        loads[name].start()

    def loaded(*names):
        for name in names:
            loads[name].wait()

    loaded("offset")
    offset = offset_ref[0]
    head_ref[pl.ds(TILE, 128 - TILE), :] = jnp.zeros((128 - TILE, WIDTH), BF16)

    cell = lax.broadcasted_iota(jnp.int32, (OWN, 1), 0)
    rest = jnp.where(cell >= TOKENS, cell - TOKENS, cell)
    line = over_twelve(rest)
    col = rest - 12 * line
    upper = col[:TOKENS] >= 12 - offset
    turned_col = col + jnp.where(cell >= TOKENS, 12, 0) + offset
    turned_col = 24 * line + jnp.where(turned_col >= 24, turned_col - 24, turned_col)
    cells = lax.broadcasted_iota(jnp.int32, (OWN, OWN), 1)
    turn = jnp.where(cells == turned_col, 1.0, 0.0).astype(BF16)
    loaded("latents")
    turned_ref[pl.ds(TOKENS, TOKENS), :] = dot_nn(turn[TOKENS:], own_ref[...]).astype(BF16)

    pl.semaphore_wait(barrier, 2 + lev_count - 1)
    halo_copies = []
    for place, side in enumerate((east, west)):
        copy = pltpu.make_async_remote_copy(
            src_ref=turned_ref.at[pl.ds(TOKENS, TOKENS)],
            dst_ref=halo_ref.at[place],
            send_sem=halo_send_sem.at[place],
            recv_sem=halo_receive_sem.at[place],
            device_id=(side, lev),
            device_id_type=mesh_id,
        )
        copy.start()
        halo_copies.append(copy)

    turned_ref[pl.ds(0, TOKENS), :] = dot_nn(turn[:TOKENS], own_ref[...]).astype(BF16)

    lane24 = lax.broadcasted_iota(jnp.int32, (24, 128), 1)
    loaded("coords", "first", "first_offset", "second", "compact")
    second_high, second_low = split(second_ref[...])
    second_both = jnp.concatenate([second_high, second_low], axis=0)
    flat_part = (
        coords_ref[:, 0:1] * first_ref[1:2, :]
        + coords_ref[:, 1:2] * first_ref[2:3, :]
        + first_offset_ref[...]
    )
    for a in range(3):
        depth_coord = float(coordinate(np.float64((1 - a) * 8.0)))
        hidden = jnp.maximum(flat_part + depth_coord * first_ref[0:1, :], 0.0)
        hidden_high, hidden_low = split(hidden)
        both = dot_nt(second_both, hidden_high)
        logits = both[:HEADS] + both[HEADS:] + dot_nt(second_high, hidden_low)
        table = (16.0 * LOG2E) / (1.0 + jnp.exp(-logits))
        for x in range(12):
            rolled = table if x == 11 else pltpu.roll(table, 256 - (11 - x), 1)
            high, low = split(rolled)
            shifted_ref[pl.ds(x * HEADS, HEADS), :] = high
            shifted_ref[pl.ds((12 + x) * HEADS, HEADS), :] = low
        spread_out = dot_nn(shifted_ref[...], compact_ref[...])
        spread_out = spread_out[:192] + spread_out[192:]
        lattice_ref[a, pl.ds(0, 192), :] = spread_out[:, :128]
        lattice_ref[a, pl.ds(192, 192), :] = spread_out[:, 128:]

    for h in range(HEADS):
        lattice = [lattice_ref[a, pl.ds(h, 24, stride=HEADS), :] for a in range(3)]
        for dz in range(2):
            for m in range(3):
                start = (4 - 2 * m) * 12
                rows = pl.ds(72 * dz + 24 * m, 24)
                near = lattice[1 - dz]
                if start:
                    near = pltpu.roll(near, 128 - start, 1)
                far = pltpu.roll(lattice[2 - dz], 72 - start, 1)
                bias_ref[h, rows, :128] = jnp.where(lane24 < 72, near, far)
                bias_ref[h, rows, 128:] = far[:, :16]

    loaded("wqkv")
    turned = turned_ref[...]
    scale = LOG2E / math.sqrt(HEAD_DIM)
    packed_ref[:, :WIDTH] = (dot_nn(turned, wqkv_ref[:, :WIDTH]) * scale).astype(BF16)
    packed_ref[:, WIDTH:] = dot_nn(turned, wqkv_ref[:, WIDTH:]).astype(BF16)

    def soft(scores):
        raised = jnp.exp2(scores - jnp.max(scores, axis=-1, keepdims=True))
        total = jnp.sum(raised, axis=-1, keepdims=True)
        return (raised * pl.reciprocal(total, approx=True)).astype(BF16)

    loaded("wproj", "post_gain", "dec_gain", "wkv", "order", "queries", "head")
    head_lane = lax.broadcasted_iota(jnp.int32, (HEADS, WIDTH), 1) // HEAD_DIM
    head_row = lax.broadcasted_iota(jnp.int32, (HEADS, WIDTH), 0)
    for i in range(8):
        query = queries_ref[pl.ds(order_ref[i], 1), :]
        level_query_ref[pl.ds(i * HEADS, HEADS), :] = jnp.where(
            head_lane == head_row, query, 0.0
        ).astype(BF16)
    expand_ref[...] = jnp.where(
        lax.broadcasted_iota(jnp.int32, (256, WIDTH), 0) % HEADS
        == lax.broadcasted_iota(jnp.int32, (256, WIDTH), 1) // HEAD_DIM,
        1.0,
        0.0,
    ).astype(BF16)
    lane48 = lax.broadcasted_iota(jnp.int32, (48, 128), 1)
    level_lane = lax.broadcasted_iota(jnp.int32, (72, 256), 1) % 128 // HEADS
    tile_copies = ([], [])

    def piece(parts):
        tile = parts[0][1]
        for start, part in parts[1:]:
            tile = jnp.where(lane48 >= start, part, tile)
        return tile

    def finish(half, groups):
        mine = pl.ds(TOKENS * half, TOKENS)
        projected = dot_nn(attended_ref[mine, :], wproj_ref[...])
        mixed = (turned_ref[mine, :].astype(F32) + post_gain_ref[...] * norm(projected)).astype(BF16)
        mixed_ref[mine, :] = mixed
        normed = (dec_gain_ref[...] * norm(mixed.astype(F32))).astype(BF16)
        keys = dot_nn(normed, wkv_ref[:, :WIDTH]).astype(BF16)
        values = dot_nn(normed, wkv_ref[:, WIDTH:]).astype(BF16).astype(F32)
        scores = dot_nt(keys, level_query_ref[...]) * (0.5 / math.sqrt(HEAD_DIM))
        upper_weight = 0.5 + 0.5 * jnp.tanh(scores[:72] - scores[72:])
        weight_high = upper_weight.astype(BF16).astype(F32)
        weight_both = jnp.concatenate([weight_high, upper_weight - weight_high], axis=1)
        value_lower = values[72:]
        value_step = values[:72] - value_lower
        for group in groups:
            targets = [lax.rem(lev + step, lev_count) for step in group]
            levels = [2 * target + j for target in targets for j in range(2)]
            picked = jnp.concatenate(
                [jnp.where(level_lane == level, weight_both, 0.0) for level in levels], axis=0
            ).astype(BF16)
            wide = dot_nn(picked, expand_ref[...])
            decoded = jnp.concatenate(
                [
                    value_lower + wide[72 * i : 72 * i + 72] * value_step
                    for i in range(len(levels))
                ],
                axis=0,
            ).astype(BF16)
            result = dot_nt(decoded, head_ref[...])
            for i, step in enumerate(group):
                result_ref[half, step] = result[TOKENS * i : TOKENS * i + TOKENS]
                slabs = []
                for x in range(3):
                    slab = result_ref[half, step, pl.ds(x, 48, stride=3), :]
                    slabs.append(pltpu.roll(slab, x * TILE % 128, 1) if x else slab)
                block = jnp.concatenate(
                    [
                        piece([(0, slabs[0]), (TILE, slabs[1])]),
                        piece([(0, slabs[1]), (2 * TILE - 128, slabs[2])]),
                    ],
                    axis=1,
                ).astype(BF16)
                if step == 0:
                    receive_ref[half, pl.ds(lev, 1)] = block[None]
                    continue
                send_ref[half, step - 1] = block
                copy = pltpu.make_async_remote_copy(
                    src_ref=send_ref.at[half, step - 1],
                    dst_ref=receive_ref.at[half, lev],
                    send_sem=tile_send_sem.at[half, step - 1],
                    recv_sem=tile_receive_sem.at[half, step - 1],
                    device_id=(lon, targets[i]),
                    device_id_type=mesh_id,
                )
                copy.start()
                tile_copies[half].append(copy)

    lane128 = lax.broadcasted_iota(jnp.int32, (TOKENS, 128), 1)
    inner = pl.ds(0, TOKENS)
    zero = jnp.zeros((), BF16)
    for quad in range(4):
        q_inner = packed_ref[inner, pl.ds(128 * quad, 128)]
        k_inner = packed_ref[inner, pl.ds(WIDTH + 128 * quad, 128)]
        v_inner = packed_ref[inner, pl.ds(2 * WIDTH + 128 * quad, 128)]
        q_heads = jnp.concatenate(
            [jnp.where(lane128 // HEAD_DIM == j, q_inner, zero) for j in range(4)], axis=0
        )
        bias = bias_ref[pl.ds(4 * quad, 4)].reshape(4 * TOKENS, TOKENS)
        heads = dot_nn(soft(dot_nt(q_heads, k_inner) + bias), v_inner)
        out = heads[:TOKENS]
        for j in range(1, 4):
            part = heads[TOKENS * j : TOKENS * j + TOKENS]
            out = jnp.where(lane128 // HEAD_DIM == j, part, out)
        attended_ref[inner, pl.ds(128 * quad, 128)] = out.astype(BF16)

    lane = lax.broadcasted_iota(jnp.int32, (1, TOKENS), 1)
    upper_key = lane - 12 * over_twelve(lane) >= 12 - offset
    side = jnp.where(upper, 1, 0) + jnp.zeros((TOKENS, TOKENS), jnp.int32)
    same = side == jnp.where(upper_key, 1, 0)
    edge = pl.ds(TOKENS, TOKENS)

    def by_head(rows):
        out = rows(0)
        for j in range(1, 4):
            out = jnp.where(lane128 // HEAD_DIM == j, rows(j), out)
        return out

    def share(quad, keys, values, met):
        query = packed_ref[edge, pl.ds(128 * quad, 128)]
        q_heads = jnp.concatenate(
            [jnp.where(lane128 // HEAD_DIM == j, query, zero) for j in range(4)], axis=0
        )
        bias = jnp.where(met[None], bias_ref[pl.ds(4 * quad, 4)], -1e30)
        scores = dot_nt(q_heads, keys) + bias.reshape(4 * TOKENS, TOKENS)
        peak = jnp.max(scores, axis=-1, keepdims=True)
        raised = jnp.exp2(scores - peak)
        total = jnp.sum(raised, axis=-1, keepdims=True)
        heads = dot_nn(raised.astype(BF16), values)
        return [
            by_head(lambda j: value[TOKENS * j : TOKENS * j + TOKENS])
            for value in (peak, total, heads)
        ]

    for quad in range(4):
        found = share(
            quad,
            packed_ref[edge, pl.ds(WIDTH + 128 * quad, 128)],
            packed_ref[edge, pl.ds(2 * WIDTH + 128 * quad, 128)],
            same,
        )
        for i in range(3):
            share_ref[i, :, pl.ds(128 * quad, 128)] = found[i]

    finish(0, ((2, 3, 1, 0),))

    for copy in halo_copies:
        copy.wait()
    halo = jnp.where(upper, halo_ref[1].astype(F32), halo_ref[0].astype(F32)).astype(BF16)
    packed_halo_ref[...] = dot_nn(halo, wqkv_ref[:, WIDTH:]).astype(BF16)
    for quad in range(4):
        lanes = pl.ds(128 * quad, 128)
        far_peak, far_total, far_out = share(
            quad,
            packed_halo_ref[:, lanes],
            packed_halo_ref[:, pl.ds(WIDTH + 128 * quad, 128)],
            jnp.logical_not(same),
        )
        near_peak = share_ref[0, :, lanes]
        peak = jnp.maximum(near_peak, far_peak)
        near_scale = jnp.exp2(near_peak - peak)
        far_scale = jnp.exp2(far_peak - peak)
        total = share_ref[1, :, lanes] * near_scale + far_total * far_scale
        out = (share_ref[2, :, lanes] * near_scale + far_out * far_scale) / total
        attended_ref[edge, lanes] = out.astype(BF16)

    finish(1, ((2, 3), (1, 0)))

    own_line = over_twelve(lax.shift_right_logical(cell, 1))
    back_col = cell - 24 * own_line - offset
    back_col = jnp.where(back_col < 0, back_col + 24, back_col)
    back_col = 12 * own_line + jnp.where(back_col >= 12, back_col + (TOKENS - 12), back_col)
    turn_back = jnp.where(cells == back_col, 1.0, 0.0).astype(BF16)
    hidden_ref[...] = dot_nn(turn_back, mixed_ref[...]).astype(BF16)

    rows = 48 * lev_count
    slot_row = lax.broadcasted_iota(jnp.int32, (48, 1), 0)
    slot = jnp.where(slot_row >= 24, 1, 0)
    lat = slot_row - 24 * slot
    source = over_twelve(2 * lat)
    base = 48 * source + 24 * slot + 4 * (lat - 6 * source)
    place = lax.broadcasted_iota(jnp.int32, (48, rows), 1) - base
    gather = jnp.concatenate([jnp.where(place == q, 1.0, 0.0) for q in range(4)], 0).astype(BF16)
    shift = TILE * offset
    count = ROW // 128
    source_lane = lax.broadcasted_iota(jnp.int32, (256, WIDTH), 0)
    step_lane = lax.broadcasted_iota(jnp.int32, (256, WIDTH), 1) - source_lane - (shift & 127)
    step_lane = jnp.where(source_lane < 3 * TILE, step_lane, -1)
    firsts = [[960 * half + 240 * q for q in range(4)] for half in range(2)]
    slides = [
        [jnp.where(step_lane == first % 128, 1.0, 0.0).astype(BF16) for first in row]
        for row in firsts
    ]
    tiles = [None] * count
    for half in range(2):
        for copy in tile_copies[half]:
            copy.wait()
        sorted_rows = dot_nn(gather, receive_ref[half].reshape(rows, 256)).astype(BF16)
        for q in range(4):
            slid = dot_nn(sorted_rows[48 * q : 48 * q + 48], slides[half][q])
            for t in range(4):
                k = (firsts[half][q] // 128 + t) % count
                part = slid[:, 128 * t : 128 * t + 128]
                tiles[k] = part if tiles[k] is None else tiles[k] + part
    whole = jnp.zeros((48, 128), jnp.int32) + lax.shift_right_logical(shift, 7)
    for bit in (1, 2, 4):
        chosen = whole & bit != 0
        tiles = [jnp.where(chosen, tiles[k - bit], tiles[k]) for k in range(count)]
    for k in range(count):
        tiles_ref[:, pl.ds(128 * k, 128)] = tiles[k].astype(BF16)


def body(
    latents,
    shift_offset,
    qkv_weight,
    proj_weight,
    post_gain,
    bias_first_weight,
    bias_first_offset,
    bias_second_weight,
    dec_gain,
    kv_weight,
    head_weight,
    level_queries,
    level_order,
):
    lon_count = lax.axis_size("lon")
    lev_count = lax.axis_size("lev")
    coords, compact = constants()
    vmem = pl.BlockSpec(memory_space=pltpu.VMEM)
    hbm = pl.BlockSpec(memory_space=pltpu.HBM)
    dma = pltpu.SemaphoreType.DMA
    hidden, tiles = pl.pallas_call(
        functools.partial(kernel, lon_count, lev_count),
        out_shape=(
            jax.ShapeDtypeStruct((OWN, WIDTH), BF16),
            jax.ShapeDtypeStruct((48, ROW), BF16),
        ),
        in_specs=[hbm] * 15,
        out_specs=(vmem, vmem),
        scratch_shapes=[
            pltpu.SMEM((1,), jnp.int32),
            pltpu.SMEM((8,), jnp.int32),
            pltpu.VMEM((OWN, WIDTH), BF16),
            pltpu.VMEM((WIDTH, 3 * WIDTH), BF16),
            pltpu.VMEM((WIDTH, WIDTH), BF16),
            pltpu.VMEM((WIDTH, 2 * WIDTH), BF16),
            pltpu.VMEM((1, WIDTH), F32),
            pltpu.VMEM((3, WIDTH), F32),
            pltpu.VMEM((1, WIDTH), F32),
            pltpu.VMEM((HEADS, WIDTH), F32),
            pltpu.VMEM((1, WIDTH), F32),
            pltpu.VMEM((128, WIDTH), BF16),
            pltpu.VMEM((8, WIDTH), F32),
            pltpu.VMEM((256, 2), F32),
            pltpu.VMEM((256, 256), BF16),
            pltpu.VMEM((OWN, WIDTH), BF16),
            pltpu.VMEM((2, TOKENS, WIDTH), BF16),
            pltpu.VMEM((384, 256), BF16),
            pltpu.VMEM((3, 384, 128), F32),
            pltpu.VMEM((HEADS, TOKENS, TOKENS), F32),
            pltpu.VMEM((OWN, 3 * WIDTH), BF16),
            pltpu.VMEM((TOKENS, 2 * WIDTH), BF16),
            pltpu.VMEM((OWN, WIDTH), BF16),
            pltpu.VMEM((3, TOKENS, WIDTH), F32),
            pltpu.VMEM((OWN, WIDTH), BF16),
            pltpu.VMEM((128, WIDTH), BF16),
            pltpu.VMEM((256, WIDTH), BF16),
            pltpu.VMEM((2, lev_count, TOKENS, 128), F32),
            pltpu.VMEM((2, lev_count - 1, 48, 256), BF16),
            pltpu.VMEM((2, lev_count, 48, 256), BF16),
            dma((15,)),
            dma((2,)),
            dma((2,)),
            dma((2, lev_count - 1)),
            dma((2, lev_count - 1)),
        ],
        compiler_params=pltpu.CompilerParams(
            collective_id=0, has_side_effects=True, vmem_limit_bytes=40 * 1024 * 1024
        ),
    )(
        shift_offset,
        *(
            pltpu.with_memory_space_constraint(value, pltpu.HBM)
            for value in (
                level_order,
                latents.reshape(OWN, WIDTH),
                qkv_weight,
                proj_weight,
                kv_weight,
                post_gain.reshape(1, WIDTH),
                bias_first_weight,
                bias_first_offset.reshape(1, WIDTH),
                bias_second_weight.T,
                dec_gain.reshape(1, WIDTH),
                head_weight.T,
                level_queries,
                jnp.asarray(coords),
                jnp.asarray(compact),
            )
        )
    )
    return hidden.reshape(latents.shape), tiles.reshape(2, 24, ROW)


def solution(mesh):
    return jax.shard_map(
        body,
        mesh=mesh,
        in_specs=(P(None, "lev", "lon", None),) + (P(),) * 12,
        out_specs=(P(None, "lev", "lon", None), P("lev", None, "lon")),
        check_vma=False,
    )
```
